512 devices in a mesh: gx: 8 (over y), gy: 8 (over z), gz: 8 (over x, core).
Axes of the slice: x: 4, y: 8, z: 8, core: 2. Of those that a mesh axis runs over, the one named last changes fastest.
Arguments:
- state: float32 [128, 128, 1024], P('gx', 'gy', 'gz'), may hold values from -6 to 6
- data_term: float32 [128, 128, 1024], P('gx', 'gy', 'gz'), may hold values from -6 to 6
- kappa: float32 [128, 128, 1024], P('gx', 'gy', 'gz'), may hold values from 0.02 to 0.5
- weight_x: float32 [128, 128, 1024], P('gx', 'gy', 'gz'), may hold values from 0.25 to 4
- weight_y: float32 [128, 128, 1024], P('gx', 'gy', 'gz'), may hold values from 0.25 to 4
- weight_z: float32 [128, 128, 1024], P('gx', 'gy', 'gz'), may hold values from 0.25 to 4
- noise_keys: int32 [4, 2, 2], replicated, may hold values from 0 to 1073741823
Outputs:
- sample: float32 [128, 128, 1024], P('gx', 'gy', 'gz')
The draws below stay inside these ranges and needn't reach their ends.
All inputs are finite; a program needn't handle non-finite values.
Results may differ from the reference program's by a relative error of at most 0.0001.
Values sent between devices are 32-bit elements; how exact they have to be, the bound alone decides.
A program may use at most 128 MiB of HBM per device.

```python
import math
import jax
import jax.numpy as jnp
from jax import lax

LEVELS = 4
SWEEPS = 2
NX = 128
NY = 128
NZ = 1024


def plant(array, stream_key, least, top_value):
    longest = array.shape.index(max(array.shape))
    spots = []
    for shift in (0, 1):
        where = [jax.random.randint(jax.random.fold_in(stream_key, axis), (), 0, length) for axis, length in enumerate(array.shape)]
        where[longest] = (where[longest] + shift) % array.shape[longest]
        spots.append(tuple(where))
    return array.at[spots[0]].set(least).at[spots[1]].set(top_value)


def shard_levels(stream_key, shape, cuts, low, largest):
    loudness, own = 1.0, jax.random.fold_in(stream_key, 6)
    for axis_at, shards_of in cuts:
        heights = jnp.exp(jax.random.uniform(jax.random.fold_in(own, axis_at), (shards_of,), jnp.float32, low / len(cuts), largest / len(cuts)))
        loudness = loudness * jnp.repeat(heights, shape[axis_at] // shards_of).reshape([-1 if axis == axis_at else 1 for axis in range(len(shape))])
    return loudness


def scatter_about(stream_key, extent, scale, reach, cuts=(), dtype=jnp.bfloat16):
    array = jax.random.normal(stream_key, extent, jnp.float32) * scale
    if len(cuts) > 0:
        array = shard_levels(stream_key, extent, cuts, -0.22, 0.18) * array
    return jnp.clip(array, min=-reach, max=reach).astype(dtype)


def setup_inputs(seed: int = 0) -> dict:
    seeds = jax.random.split(jax.random.key(seed), 8)
    state = scatter_about(seeds[0], (NX, NY, NZ), 1.0, 6.0, ((0, 8), (1, 8), (2, 8)), jnp.float32)
    data_term = scatter_about(seeds[1], (NX, NY, NZ), 1.0, 6.0, ((0, 8), (1, 8), (2, 8)), jnp.float32)
    kappa = jnp.clip(jnp.exp(math.log(0.5) - 3.218876 * jax.random.uniform(seeds[2], (NX, NY, NZ), jnp.float32) ** shard_levels(seeds[2], (NX, NY, NZ), ((0, 8), (1, 8), (2, 8)), -0.2, 0.2)), 0.02, 0.5)
    weight_x = jnp.clip(jnp.exp(math.log(4.0) - 2.7725887 * jax.random.uniform(seeds[3], (NX, NY, NZ), jnp.float32) ** shard_levels(seeds[3], (NX, NY, NZ), ((0, 8), (1, 8), (2, 8)), -0.2, 0.2)), 0.25, 4.0)
    weight_y = jnp.clip(jnp.exp(math.log(4.0) - 2.7725887 * jax.random.uniform(seeds[4], (NX, NY, NZ), jnp.float32) ** shard_levels(seeds[4], (NX, NY, NZ), ((0, 8), (1, 8), (2, 8)), -0.2, 0.2)), 0.25, 4.0)
    weight_z = jnp.clip(jnp.exp(math.log(4.0) - 2.7725887 * jax.random.uniform(seeds[5], (NX, NY, NZ), jnp.float32) ** shard_levels(seeds[5], (NX, NY, NZ), ((0, 8), (1, 8), (2, 8)), -0.2, 0.2)), 0.25, 4.0)
    noise_keys = plant(jax.random.randint(seeds[6], (LEVELS, 2, SWEEPS), 0, 1073741824), jax.random.fold_in(seeds[6], 1), 0, 1073741823).astype(jnp.int32)
    return dict(state=state, data_term=data_term, kappa=kappa, weight_x=weight_x, weight_y=weight_y, weight_z=weight_z, noise_keys=noise_keys)


def mixing(h):
    h = h ^ lax.shift_right_logical(h, jnp.int32(16))
    h = h * jnp.int32(-2048144789)
    h = h ^ lax.shift_right_logical(h, jnp.int32(13))
    h = h * jnp.int32(-1028477387)
    h = h ^ lax.shift_right_logical(h, jnp.int32(16))
    return h

def gaussian_like(index, key):
    first = mixing(index * jnp.int32(-1640531535) ^ key)
    second = mixing(first ^ jnp.int32(1759714724))
    scale = 1.0 / 16777216.0
    upper = lax.shift_right_logical(first, jnp.int32(8)).astype(jnp.float32) * scale
    lower = lax.shift_right_logical(second, jnp.int32(8)).astype(jnp.float32) * scale
    return (upper + lower - 1.0) * math.sqrt(6.0)

def cell_numbers(shape, offsets, whole):
    first = lax.broadcasted_iota(jnp.int32, shape, 0) + offsets[0]
    second = lax.broadcasted_iota(jnp.int32, shape, 1) + offsets[1]
    third = lax.broadcasted_iota(jnp.int32, shape, 2) + offsets[2]
    index = (first * whole[1] + second) * whole[2] + third
    red = first + second + third & 1 == 0
    return (index, red)

def coarsen(kappa, weight_x, weight_y, weight_z):
    a, b, c = kappa.shape
    blocks = (a // 2, 2, b // 2, 2, c // 2, 2)
    kappa_c = kappa.reshape(blocks).sum((1, 3, 5))
    wx_c = weight_x.reshape(blocks)[:, 1].sum((2, 4))
    wy_c = weight_y.reshape(blocks)[:, :, :, 1].sum((1, 4))
    wz_c = weight_z.reshape(blocks)[..., 1].sum((1, 3))
    return (kappa_c, wx_c, wy_c, wz_c)

def restrict(field):
    a, b, c = field.shape
    return field.reshape(a // 2, 2, b // 2, 2, c // 2, 2).sum((1, 3, 5))

def prolong(field):
    a, b, c = field.shape
    spread = jnp.broadcast_to(field[:, None, :, None, :, None], (a, 2, b, 2, c, 2))
    return spread.reshape(2 * a, 2 * b, 2 * c)

def lower_neighbours(weight_x, weight_y, weight_z):
    wxm = jnp.pad(weight_x, ((1, 0), (0, 0), (0, 0)))[:-1]
    wym = jnp.pad(weight_y, ((0, 0), (1, 0), (0, 0)))[:, :-1]
    wzm = jnp.pad(weight_z, ((0, 0), (0, 0), (1, 0)))[:, :, :-1]
    return (wxm, wym, wzm)

def finish(kappa, wx, wy, wz, wxm, wym, wzm):
    diag = kappa + wx + wxm + wy + wym + wz + wzm
    return (kappa, wx, wy, wz, wxm, wym, wzm, diag)

def stencil_sum(padded, coef):
    wx, wy, wz, wxm, wym, wzm = (coef[1], coef[2], coef[3], coef[4], coef[5], coef[6])
    total = wx * padded[2:, 1:-1, 1:-1] + wxm * padded[:-2, 1:-1, 1:-1]
    total = total + wy * padded[1:-1, 2:, 1:-1] + wym * padded[1:-1, :-2, 1:-1]
    total = total + wz * padded[1:-1, 1:-1, 2:] + wzm * padded[1:-1, 1:-1, :-2]
    return total

def sweep(field, rhs, coef, index, red, key, pad_fn):
    diag = coef[7]
    shaken = gaussian_like(index, key) * lax.rsqrt(diag)
    for mask in (red, jnp.logical_not(red)):
        padded = pad_fn(field)
        fresh = (rhs + stencil_sum(padded, coef)) / diag + shaken
        field = jnp.where(mask, fresh, field)
    return field

def plain_pad(field):
    return jnp.pad(field, 1)

def reference(state, data_term, kappa, weight_x, weight_y, weight_z, noise_keys):
    raw = [(kappa, weight_x, weight_y, weight_z)]
    for level in range(1, LEVELS):
        raw.append(coarsen(*raw[-1]))

    def cycle(level, field, rhs):
        kap, wx, wy, wz = raw[level]
        coef = finish(kap, wx, wy, wz, *lower_neighbours(wx, wy, wz))
        index, red = cell_numbers(field.shape, (0, 0, 0), field.shape)
        for step in range(SWEEPS):
            field = sweep(field, rhs, coef, index, red, noise_keys[level, 0, step], plain_pad)
        if level + 1 < LEVELS:
            residual = rhs - (coef[7] * field - stencil_sum(plain_pad(field), coef))
            coarse_rhs = restrict(residual)
            coarse = cycle(level + 1, jnp.zeros(coarse_rhs.shape, jnp.float32), coarse_rhs)
            field = field + prolong(coarse)
        for step in range(SWEEPS):
            field = sweep(field, rhs, coef, index, red, noise_keys[level, 1, step], plain_pad)
        return field
    return cycle(0, state, data_term)
```

```python
import functools
import math

import jax
import jax.numpy as jnp
from jax import lax
from jax.experimental import pallas as pl
from jax.experimental.pallas import tpu as pltpu
from jax.sharding import PartitionSpec as P

AXES = ("gx", "gy", "gz")
MESH = pl.DeviceIdType.MESH
F32 = jnp.float32
SHARDS = 8
GRID = ((128, 128, 1024), (64, 64, 512), (32, 32, 256), (16, 16, 128))
X = (28, 20, 40, 18)
S = (32, 24, 32, 16)
W = (256, 128, 128, 128)
HX = (6, 6, 4, 1)
HY = (8, 8, 0, 0)


def neighbour(**moves):
    return {a: lax.rem(lax.axis_index(a) + (m + SHARDS), SHARDS) for a, m in moves.items() if m}


def dot(a, b):
    return jnp.dot(a, b, precision=lax.Precision.HIGHEST, preferred_element_type=F32)


def iota(shape, dim):
    return lax.broadcasted_iota(jnp.int32, shape, dim)


def mixing(h):
    h = h ^ lax.shift_right_logical(h, jnp.int32(16))
    h = h * jnp.int32(-2048144789)
    h = h ^ lax.shift_right_logical(h, jnp.int32(13))
    h = h * jnp.int32(-1028477387)
    h = h ^ lax.shift_right_logical(h, jnp.int32(16))
    return h


def gaussian_like(index, key):
    first = mixing(index * jnp.int32(-1640531535) ^ key)
    second = mixing(first ^ jnp.int32(1759714724))
    scale = 1.0 / 16777216.0
    upper = lax.shift_right_logical(first, jnp.int32(8)).astype(F32) * scale
    lower = lax.shift_right_logical(second, jnp.int32(8)).astype(F32) * scale
    return (upper + lower - 1.0) * math.sqrt(6.0)


def relative_z(level, shape):
    lane = iota(shape, len(shape) - 1)
    if level == 0:
        return jnp.where(lane < 192, lane, lane - 256)
    if level == 1:
        return jnp.where(lane < 96, lane, lane - 128)
    return lane - (32 if level == 2 else 16)


def x_global(level, x):
    n = GRID[level][0]
    start = lax.axis_index("gx") * (n // SHARDS) if level < 2 else 0
    return (start + x - HX[level] + n) & (n - 1)


def yz_global(level):
    shape = (S[level], W[level])
    ny, nz = GRID[level][1:]
    start = lax.axis_index("gy") * (ny // SHARDS) if level < 2 else 0
    y = (iota(shape, 0) + (start - HY[level] + ny)) & (ny - 1)
    z = (relative_z(level, shape) + (lax.axis_index("gz") * (nz // SHARDS) + nz)) & (nz - 1)
    return y, z


def fill_noise(level, out, keys, base):
    nx, ny, nz = GRID[level]
    y, z = yz_global(level)
    plane = y * nz + z

    def row(x, c):
        index = plane + x_global(level, x) * (ny * nz)
        for s in range(4):
            out[s, x] = gaussian_like(index, keys[base + s])
        return c

    lax.fori_loop(*inner(level), row, 0)


def inner(level, shrink=0):
    if level >= 2:
        return HX[level], X[level] - HX[level]
    return 1 + shrink, X[level] - 1 - shrink


def derive(level, kap, wx, wy, wz, a, noise):
    nx, ny, nz = GRID[level]
    y, z = yz_global(level)
    y_first, y_last, z_first, z_last = y == 0, y == ny - 1, z == 0, z == nz - 1
    s, w = S[level], W[level]

    def row(x, c):
        xg = x_global(level, x)
        up, vp, sp = wx[x], wy[x], wz[x]
        um = jnp.where(xg == 0, 0.0, wx[x - 1])
        vm = jnp.where(y_first, 0.0, pltpu.roll(vp, 1, 0))
        sm = jnp.where(z_first, 0.0, pltpu.roll(sp, 1, 1))
        diag = kap[x] + up + um + vp + vm + sp + sm
        good = diag > 0.0
        inv = jnp.where(good, 1.0 / diag, 0.0)
        root = jnp.where(good, lax.rsqrt(diag), 0.0)
        a[0, x] = jnp.where(xg == nx - 1, 0.0, up) * inv
        a[1, x] = um * inv
        a[2, x] = jnp.where(y_last, 0.0, vp) * inv
        a[3, x] = vm * inv
        a[4, x] = jnp.where(z_last, 0.0, sp) * inv
        a[5, x] = sm * inv
        a[6, x] = diag
        a[7, x] = inv
        for i in range(4):
            noise[i, x] = noise[i, x] * root
        return c

    lax.fori_loop(*inner(level), row, 0)


def scale_rhs(level, rhs, a):
    def row(x, c):
        rhs[x] = rhs[x] * a[7, x]
        return c

    lax.fori_loop(*inner(level), row, 0)


def around(level, f, a, x):
    v = f[x]
    s, w = S[level], W[level]
    t = a[0, x] * f[x + 1] + a[1, x] * f[x - 1]
    t = t + a[2, x] * pltpu.roll(v, s - 1, 0) + a[3, x] * pltpu.roll(v, 1, 0)
    t = t + a[4, x] * pltpu.roll(v, w - 1, 1) + a[5, x] * pltpu.roll(v, 1, 1)
    return v, t


def half_sweep(level, f, rhs, a, noise, sweep, color, shrink):
    shape = (S[level], W[level])
    yz = iota(shape, 0) + iota(shape, 1)

    def row(x, c):
        v, t = around(level, f, a, x)
        fresh = rhs[x] + t + noise[sweep, x]
        odd = (yz + (x + (HX[level] + HY[level]))) & 1
        f[x] = jnp.where(odd == color, fresh, v)
        return c

    lax.fori_loop(*inner(level, shrink), row, 0)


def first_half(level, f, rhs, noise, sweep, shrink):
    shape = (S[level], W[level])
    yz = iota(shape, 0) + iota(shape, 1)

    def row(x, c):
        fresh = rhs[x] + noise[sweep, x]
        odd = (yz + (x + (HX[level] + HY[level]))) & 1
        f[x] = jnp.where(odd == 0, fresh, 0.0)
        return c

    lax.fori_loop(*inner(level, shrink), row, 0)


def sweeps(level, f, rhs, a, noise, leg, shrinks, from_zero=False):
    for i in range(4):
        if from_zero and i == 0:
            first_half(level, f, rhs, noise, 0, shrinks[0])
        else:
            half_sweep(level, f, rhs, a, noise, 2 * leg + i // 2, i % 2, shrinks[i])


def residual(level, f, rhs, a, out, x0, x1, y0, y1):
    def row(x, c):
        v, t = around(level, f, a, x)
        r = a[6, x] * (rhs[x] + t - v)
        out[x - x0, pl.ds(0, y1 - y0), :] = r[y0:y1, 0:128]
        return c

    lax.fori_loop(x0, x1, row, 0)


def pairs(ref, cx, y0, n, xs=(0, 1), ys=(0, 1)):
    total = None
    for dx in xs:
        for dy in ys:
            v = ref[2 * cx + dx, pl.ds(y0 + dy, n, stride=2), :]
            total = v if total is None else total + v
    return total


def halve(rows, cols, start_r, limit, start_c, odd=False):
    r, c = iota((rows, cols), 0) - start_r, iota((rows, cols), 1) - start_c
    hit = (lax.shift_right_arithmetic(r, 1) == c) & (r >= 0) & (r < limit)
    if odd:
        hit = hit & (r & 1 == 1)
    return hit.astype(F32)


class Halo:
    def __init__(self, level, field, depth, packs, sems):
        self.level, self.field, self.depth = level, field, depth
        self.send_up, self.send_down, self.got_up, self.got_down = packs
        self.ssem, self.rsem = sems
        self.n = GRID[level][0] // SHARDS
        self.lanes = GRID[level][2] // SHARDS

    def plane_copies(self):
        n, d, hx, hy = self.n, self.depth, HX[self.level], HY[self.level]
        out = []
        moves = [(1, 0), (-1, 0), (0, 1), (0, -1), (1, 1), (1, -1), (-1, 1), (-1, -1)]
        for i, (mx, my) in enumerate(moves):
            sx, dx, lx = {0: (hx, hx, n), 1: (hx + n - d, hx - d, d), -1: (hx, hx + n, d)}[mx]
            sy, dy, ly = {0: (hy, hy, n), 1: (hy + n - 8, hy - 8, 8), -1: (hy, hy + n, 8)}[my]
            out.append(pltpu.make_async_remote_copy(
                src_ref=self.field.at[:, pl.ds(sx, lx), pl.ds(sy, ly), pl.ds(0, 128)],
                dst_ref=self.field.at[:, pl.ds(dx, lx), pl.ds(dy, ly), pl.ds(0, 128)],
                send_sem=self.ssem.at[i], recv_sem=self.rsem.at[i],
                device_id=neighbour(gx=mx, gy=my), device_id_type=MESH))
        return out

    def depth_copies(self):
        out = []
        for i, (mz, src, dst) in enumerate(((1, self.send_up, self.got_up), (-1, self.send_down, self.got_down))):
            out.append(pltpu.make_async_remote_copy(
                src_ref=src, dst_ref=dst, send_sem=self.ssem.at[8 + i], recv_sem=self.rsem.at[8 + i],
                device_id=neighbour(gz=mz), device_id_type=MESH))
        return out

    def plane_start(self):
        for c in self.plane_copies():
            c.start()

    def plane_wait(self):
        for c in self.plane_copies():
            c.wait_recv()
        for c in self.plane_copies():
            c.wait_send()

    def depth_start(self):
        st = S[self.level] // 8
        groups = X[self.level] // 4
        n = self.lanes
        lane = iota((8, 128), 1)

        def pack(i, c):
            f, g = i // groups, i % groups
            up = down = jnp.zeros((8, 128), F32)
            for k in range(4 * st):
                v = self.field[f, 4 * g + k // st, pl.ds(8 * (k % st), 8), pl.ds(0, 128)]
                here = lax.shift_right_logical(lane, 3) == k
                up = jnp.where(here, pltpu.roll(v, (8 * k - (n - 8)) % 128, 1), up)
                down = jnp.where(here, pltpu.roll(v, (8 * k) % 128, 1), down)
            self.send_up[f, g] = up
            self.send_down[f, g] = down
            return c

        lax.fori_loop(0, groups * self.field.shape[0], pack, 0)
        for c in self.depth_copies():
            c.start()

    def depth_wait(self):
        for c in self.depth_copies():
            c.wait_recv()
        for c in self.depth_copies():
            c.wait_send()
        st = S[self.level] // 8
        groups = X[self.level] // 4
        lane = iota((8, 128), 1)
        fine = self.level == 0
        at = 0 if fine else self.lanes

        def unpack(i, c):
            f, g = i // groups, i % groups
            below, above = self.got_up[f, g], self.got_down[f, g]
            for k in range(4 * st):
                rows = pl.ds(8 * (k % st), 8)
                x = 4 * g + k // st
                low = pltpu.roll(below, (120 - 8 * k) % 128, 1)
                high = pltpu.roll(above, (at - 8 * k) % 128, 1)
                both = jnp.where(lane < 96, high, low)
                if fine:
                    self.field[f, x, rows, pl.ds(128, 128)] = both
                else:
                    own = self.field[f, x, rows, pl.ds(0, 128)]
                    self.field[f, x, rows, pl.ds(0, 128)] = jnp.where(lane < 64, own, both)
            return c

        lax.fori_loop(0, groups * self.field.shape[0], unpack, 0)


class Gather:
    def __init__(self, by_x, by_xy, plane, below, above, sems):
        self.by_x, self.by_xy, self.plane, self.below, self.above = by_x, by_xy, plane, below, above
        self.ssem, self.rsem = sems

    def ring(self, axis, src, dst, base):
        out = []
        me = lax.axis_index(axis)
        for i, m in enumerate((1, 7, 2, 6, 3, 5, 4)):
            out.append(pltpu.make_async_remote_copy(
                src_ref=src, dst_ref=dst.at[me], send_sem=self.ssem.at[base + i], recv_sem=self.rsem.at[base + i],
                device_id={axis: lax.rem(me + m, SHARDS)}, device_id_type=MESH))
        return out

    def x_copies(self):
        return self.ring("gx", self.by_x.at[lax.axis_index("gx")], self.by_x, 0)

    def y_copies(self):
        return self.ring("gy", self.by_xy.at[lax.axis_index("gy")], self.by_xy, 7)

    def z_copies(self):
        return [
            pltpu.make_async_remote_copy(
                src_ref=self.plane, dst_ref=dst, send_sem=self.ssem.at[14 + i], recv_sem=self.rsem.at[14 + i],
                device_id=neighbour(gz=m), device_id_type=MESH)
            for i, (m, dst) in enumerate(((1, self.below), (-1, self.above)))]

    def wait(self, copies):
        for c in copies:
            c.wait_recv()
        for c in copies:
            c.wait_send()

    def x_start(self):
        for c in self.x_copies():
            c.start()

    def y_start(self):
        self.wait(self.x_copies())
        me = lax.axis_index("gy")
        for i in range(SHARDS):
            self.by_xy[me, i] = self.by_x[i]
        for c in self.y_copies():
            c.start()

    def z_start(self):
        self.wait(self.y_copies())

        def put(i, c):
            gx, gy = i // SHARDS, i % SHARDS
            for f in range(self.plane.shape[0]):
                self.plane[f, gx, pl.ds(4 * gy, 4), :] = self.by_xy[gy, gx, f]
            return c

        lax.fori_loop(0, SHARDS * SHARDS, put, 0)
        for c in self.z_copies():
            c.start()

    def finish(self, outs):
        self.wait(self.z_copies())
        lane = iota((32, 128), 1)

        def put(gx, c):
            for f, out in enumerate(outs):
                own, low, high = self.plane[f, gx], self.below[f, gx], self.above[f, gx]
                for xx in range(4):
                    v = jnp.where(lane < 32, pltpu.roll(low, (-32 * xx) % 128, 1),
                                  jnp.where(lane < 64, pltpu.roll(own, (32 - 32 * xx) % 128, 1),
                                            jnp.where(lane < 96, pltpu.roll(high, (64 - 32 * xx) % 128, 1), 0.0)))
                    out[HX[2] + 4 * gx + xx] = v
            return c

        lax.fori_loop(0, SHARDS, put, 0)


def kernel(keys, state, data, kappa, weight_x, weight_y, weight_z, out,
           f0, xd0, a0, n0, c1, r1, f1, xd1, a1, n1, c2, r2, f2, a2, n2, c3, r3, f3, a3, n3,
           res, t64, t256,
           p0a, p0b, p0c, p0d, pxa, pxb, pxc, pxd, pca, pcb, pcc, pcd, pra, prb, prc, prd, pya, pyb, pyc, pyd,
           gcx, gcxy, gcp, gcl, gch, grx, grxy, grp, grl, grh,
           ssem, rsem):
    def sems(i):
        return ssem.at[i], rsem.at[i]

    bar = pltpu.get_barrier_semaphore()

    for ref in (f0, xd0, c1, r1, xd1):
        def clear(i, c, ref=ref):
            ref[i // ref.shape[1], i % ref.shape[1]] = jnp.zeros(ref.shape[2:], F32)
            return c
        lax.fori_loop(0, ref.shape[0] * ref.shape[1], clear, 0)
    for ref in (f1, f2, f3, r2, r3):
        def wipe(i, c, ref=ref):
            ref[i] = jnp.zeros(ref.shape[1:], F32)
            return c
        lax.fori_loop(0, ref.shape[0], wipe, 0)
    for ref, rows in ((c2, X[2]), (c3, X[3])):
        ref[1, HX[2] - 1 if ref is c2 else 0] = jnp.zeros(ref.shape[2:], F32)

    for i, ref in enumerate((state, data, kappa, weight_x, weight_y, weight_z)):
        def load(x, c, i=i, ref=ref):
            f0[i, HX[0] + x, pl.ds(8, 16), pl.ds(0, 128)] = ref[x]
            return c
        lax.fori_loop(0, 16, load, 0)

    partners = [{"gx": m} for m in range(1, 8)] + [{"gy": m} for m in range(1, 8)] + [{"gz": 1}, {"gz": -1}]
    partners += [{"gx": a, "gy": b} for a in (1, -1) for b in (1, -1)]
    for p in partners:
        pl.semaphore_signal(bar, inc=1, device_id=neighbour(**p), device_id_type=MESH)
    pl.semaphore_wait(bar, len(partners))

    halo0 = Halo(0, f0, 5, (p0a, p0b, p0c, p0d), sems(0))
    halox0 = Halo(0, xd0, 4, (pxa, pxb, pxc, pxd), sems(1))
    haloc1 = Halo(1, c1, 6, (pca, pcb, pcc, pcd), sems(2))
    halor1 = Halo(1, r1, 6, (pra, prb, prc, prd), sems(3))
    halox1 = Halo(1, xd1, 6, (pya, pyb, pyc, pyd), sems(4))
    gatherc = Gather(gcx, gcxy, gcp, gcl, gch, sems(5))
    gatherr = Gather(grx, grxy, grp, grl, grh, sems(6))

    halo0.plane_start()

    m01, m01_odd = halve(128, 128, 0, 128, 0), halve(128, 128, 0, 128, 0, True)
    both, odd = (0, 1), (1,)
    for i, (ref, xs, ys, m) in enumerate(((kappa, both, both, m01), (weight_x, odd, both, m01),
                                          (weight_y, both, odd, m01), (weight_z, both, both, m01_odd))):
        for cx in range(8):
            t64[pl.ds(8 * cx, 8), :] = pairs(ref, cx, 0, 8, xs, ys)
        t = dot(t64[...], m)
        for cx in range(8):
            c1[i, HX[1] + cx, pl.ds(8, 8), :] = t[8 * cx:8 * cx + 8]
    haloc1.plane_start()
    gx = lax.axis_index("gx")
    for i, (xs, ys, flag) in enumerate(((both, both, False), (odd, both, False), (both, odd, False), (both, both, True))):
        t = jnp.zeros((4, 128), F32)
        for cx in range(4):
            t = t + dot(pairs(c1.at[i], 3 + cx, 8, 4, xs, ys), halve(128, 128, 0, 64, 32 * cx, flag))
        gcx[gx, i] = t
    gatherc.x_start()

    fill_noise(0, n0, keys, 0)
    halo0.plane_wait()
    halo0.depth_start()
    haloc1.plane_wait()
    haloc1.depth_start()
    gatherc.y_start()
    fill_noise(1, n1, keys, 4)
    halo0.depth_wait()

    x0, b0 = f0.at[0], f0.at[1]
    derive(0, f0.at[2], f0.at[3], f0.at[4], f0.at[5], a0, n0)
    scale_rhs(0, b0, a0)
    sweeps(0, x0, b0, a0, n0, 0, (1, 2, 3, 4))
    residual(0, x0, b0, a0, res, HX[0], HX[0] + 16, 8, 24)
    for cx in range(8):
        t64[pl.ds(8 * cx, 8), :] = pairs(res, cx, 0, 8)
    t = dot(t64[...], m01)
    for cx in range(8):
        r1[0, HX[1] + cx, pl.ds(8, 8), :] = t[8 * cx:8 * cx + 8]
    halor1.plane_start()

    def keep0(x, c):
        xd0[0, x, pl.ds(8, 16), pl.ds(0, 128)] = x0[x, pl.ds(8, 16), pl.ds(0, 128)]
        return c
    lax.fori_loop(HX[0], HX[0] + 16, keep0, 0)
    halox0.plane_start()
    haloc1.depth_wait()
    derive(1, c1.at[0], c1.at[1], c1.at[2], c1.at[3], a1, n1)
    halor1.plane_wait()
    halor1.depth_start()
    gatherc.z_start()
    halox0.plane_wait()
    halox0.depth_start()
    fill_noise(2, n2, keys, 8)
    fill_noise(3, n3, keys, 12)
    halor1.depth_wait()

    b1 = r1.at[0]
    scale_rhs(1, b1, a1)
    sweeps(1, f1, b1, a1, n1, 0, (0, 1, 2, 3), True)
    residual(1, f1, b1, a1, res, HX[1], HX[1] + 8, 8, 16)
    t = jnp.zeros((4, 128), F32)
    for cx in range(4):
        t = t + dot(pairs(res, cx, 0, 4), halve(128, 128, 0, 64, 32 * cx))
    grx[gx, 0] = t
    gatherr.x_start()

    def keep1(x, c):
        xd1[0, x, pl.ds(8, 8), :] = f1[x, pl.ds(8, 8), :]
        return c
    lax.fori_loop(HX[1], HX[1] + 8, keep1, 0)
    halox1.plane_start()
    gatherc.finish([c2.at[i] for i in range(4)])
    derive(2, c2.at[0], c2.at[1], c2.at[2], c2.at[3], a2, n2)
    gatherr.y_start()
    halox1.plane_wait()
    halox1.depth_start()
    m23, m23_odd = halve(128, 128, 0, 96, 0), halve(128, 128, 0, 96, 0, True)
    for i, (xs, ys, m) in enumerate(((both, both, m23), (odd, both, m23), (both, odd, m23), (both, both, m23_odd))):
        for cx in range(16):
            t256[pl.ds(16 * cx, 16), :] = pairs(c2.at[i], 2 + cx, 0, 16, xs, ys)
        t = dot(t256[...], m)
        for cx in range(16):
            c3[i, HX[3] + cx] = t[16 * cx:16 * cx + 16]
    derive(3, c3.at[0], c3.at[1], c3.at[2], c3.at[3], a3, n3)
    halox0.depth_wait()
    gatherr.z_start()
    halox1.depth_wait()
    gatherr.finish([r2])

    scale_rhs(2, r2, a2)
    sweeps(2, f2, r2, a2, n2, 0, (0, 0, 0, 0), True)
    residual(2, f2, r2, a2, res, HX[2], HX[2] + 32, 0, 32)
    for cx in range(16):
        t256[pl.ds(16 * cx, 16), :] = pairs(res, cx, 0, 16)
    t = dot(t256[...], m23)
    for cx in range(16):
        r3[HX[3] + cx] = t[16 * cx:16 * cx + 16]
    scale_rhs(3, r3, a3)
    sweeps(3, f3, r3, a3, n3, 0, (0, 0, 0, 0), True)
    sweeps(3, f3, r3, a3, n3, 1, (0, 0, 0, 0))
    for cx in range(16):
        t256[pl.ds(16 * cx, 16), :] = f3[HX[3] + cx]
    i3, i2 = iota((128, 128), 0), iota((128, 128), 1)
    t = dot(t256[...], ((lax.shift_right_logical(i2, 1) == i3) & (i2 < 96)).astype(F32))
    for cx in range(16):
        for dx in both:
            for dy in both:
                rows = pl.ds(dy, 16, stride=2)
                x = HX[2] + 2 * cx + dx
                f2[x, rows, :] = f2[x, rows, :] + t[16 * cx:16 * cx + 16]
    sweeps(2, f2, r2, a2, n2, 1, (0, 0, 0, 0))

    gy = lax.axis_index("gy")
    z1 = relative_z(1, (128, 128))
    m21 = ((i3 == lax.shift_right_arithmetic(z1, 1) + 32) & (z1 >= -6) & (z1 < 70)).astype(F32)
    for j in range(10):
        v = f2[HX[2] + 4 * gx + (j - 3)]
        t256[pl.ds(16 * j, 16), :] = pltpu.roll(v, lax.rem(36 - 4 * gy, 32), 0)[:16]
    t = dot(t256[...], m21)
    for j in range(10):
        for dx in both:
            for dy in both:
                rows = pl.ds(dy, 12, stride=2)
                x = 2 * j + dx
                xd1[0, x, rows, :] = xd1[0, x, rows, :] + t[16 * j:16 * j + 12]
    sweeps(1, xd1.at[0], b1, a1, n1, 1, (0, 1, 2, 3))

    z0 = relative_z(0, (128, 256))
    hit = iota((128, 256), 0) == (lax.shift_right_arithmetic(z0, 1) & 127)
    m10 = (hit & (z0 >= -4) & (z0 < 132)).astype(F32)
    for j in range(12):
        t256[pl.ds(16 * j, 16), :] = xd1[0, 4 + j, pl.ds(4, 16), :]
    t = dot(t256[pl.ds(0, 192), :], m10)
    for j in range(12):
        for dy in both:
            rows = pl.ds(dy, 16, stride=2)
            res[j, rows, :] = t[16 * j:16 * j + 16, :128]
            res[16 + j, rows, :] = t[16 * j:16 * j + 16, 128:]

    def add(j, c):
        for dx in both:
            x = 2 + 2 * j + dx
            xd0[0, x, :, pl.ds(0, 128)] = xd0[0, x, :, pl.ds(0, 128)] + res[j]
            xd0[0, x, :, pl.ds(128, 128)] = xd0[0, x, :, pl.ds(128, 128)] + res[16 + j]
        return c
    lax.fori_loop(0, 12, add, 0)
    sweeps(0, xd0.at[0], b0, a0, n0, 1, (2, 3, 4, 5))

    def give(x, c):
        out[x] = xd0[0, HX[0] + x, pl.ds(8, 16), pl.ds(0, 128)]
        return c
    lax.fori_loop(0, 16, give, 0)


def level_scratch(level, fields):
    shape = (X[level], S[level], W[level])
    return [pltpu.VMEM((n,) + shape if n else shape, F32) for n in fields]


def packs(level, n):
    return [pltpu.VMEM((n, X[level] // 4, 8, 128), F32)] * 4


def gathers(n):
    return [pltpu.VMEM((8, n, 4, 128), F32), pltpu.VMEM((8, 8, n, 4, 128), F32)] + [
        pltpu.VMEM((n, 8, 32, 128), F32)] * 3


def per_device(state, data_term, kappa, weight_x, weight_y, weight_z, noise_keys):
    scratch = (
        level_scratch(0, (6, 1, 8, 4)) + level_scratch(1, (4, 1, 0, 1, 8, 4))
        + level_scratch(2, (4, 0, 0, 8, 4)) + level_scratch(3, (4, 0, 0, 8, 4))
        + [pltpu.VMEM((32, 32, 128), F32), pltpu.VMEM((64, 128), F32), pltpu.VMEM((256, 128), F32)]
        + packs(0, 6) + packs(0, 1) + packs(1, 4) + packs(1, 1) + packs(1, 1)
        + gathers(4) + gathers(1)
        + [pltpu.SemaphoreType.DMA((7, 16)), pltpu.SemaphoreType.DMA((7, 16))])
    return pl.pallas_call(
        kernel,
        out_shape=jax.ShapeDtypeStruct(state.shape, F32),
        in_specs=[pl.BlockSpec(memory_space=pltpu.SMEM)] + [pl.BlockSpec(memory_space=pltpu.VMEM)] * 6,
        out_specs=pl.BlockSpec(memory_space=pltpu.VMEM),
        scratch_shapes=scratch,
        compiler_params=pltpu.CompilerParams(
            collective_id=0, has_side_effects=True, vmem_limit_bytes=56 * 2**20),
    )(noise_keys.reshape(16), state, data_term, kappa, weight_x, weight_y, weight_z)


def solution(mesh):
    spec = P(*AXES)
    return jax.shard_map(
        per_device, mesh=mesh, in_specs=(spec,) * 6 + (P(),), out_specs=spec, check_vma=False)
```

```python
import functools
import math

import jax
import jax.numpy as jnp
from jax import lax
from jax.experimental import pallas as pl
from jax.experimental.pallas import tpu as pltpu
from jax.sharding import PartitionSpec as P

AXES = ("gx", "gy", "gz")
MESH = pl.DeviceIdType.MESH
F32 = jnp.float32
SHARDS = 8
GRID = ((128, 128, 1024), (64, 64, 512), (32, 32, 256), (16, 16, 128))
X = (28, 20, 40, 18)
S = (32, 24, 32, 16)
W = (256, 128, 128, 128)
HX = (6, 6, 4, 1)
HY = (8, 8, 0, 0)


def neighbour(**moves):
    return {a: lax.rem(lax.axis_index(a) + (m + SHARDS), SHARDS) for a, m in moves.items() if m}


def dot(a, b):
    return jnp.dot(a, b, precision=lax.Precision.HIGHEST, preferred_element_type=F32)


def iota(shape, dim):
    return lax.broadcasted_iota(jnp.int32, shape, dim)


def mixing(h):
    h = h ^ lax.shift_right_logical(h, jnp.int32(16))
    h = h * jnp.int32(-2048144789)
    h = h ^ lax.shift_right_logical(h, jnp.int32(13))
    h = h * jnp.int32(-1028477387)
    h = h ^ lax.shift_right_logical(h, jnp.int32(16))
    return h


def gaussian_like(index, key):
    first = mixing(index * jnp.int32(-1640531535) ^ key)
    second = mixing(first ^ jnp.int32(1759714724))
    steps = lax.shift_right_logical(first, jnp.int32(8)) + lax.shift_right_logical(second, jnp.int32(8))
    return steps.astype(F32) * (math.sqrt(6.0) / 16777216.0) - math.sqrt(6.0)


def relative_z(level, shape):
    lane = iota(shape, len(shape) - 1)
    if level == 0:
        return jnp.where(lane < 192, lane, lane - 256)
    if level == 1:
        return jnp.where(lane < 96, lane, lane - 128)
    return lane - (32 if level == 2 else 16)


def x_global(level, x):
    n = GRID[level][0]
    start = lax.axis_index("gx") * (n // SHARDS) if level < 2 else 0
    return (start + x - HX[level] + n) & (n - 1)


def yz_global(level):
    shape = (S[level], W[level])
    ny, nz = GRID[level][1:]
    start = lax.axis_index("gy") * (ny // SHARDS) if level < 2 else 0
    y = (iota(shape, 0) + (start - HY[level] + ny)) & (ny - 1)
    z = (relative_z(level, shape) + (lax.axis_index("gz") * (nz // SHARDS) + nz)) & (nz - 1)
    return y, z


def blocks(lo, count, size, body):
    def step(i, c):
        for ref, at, value in body(lo + i * size):
            ref[at] = value
        return c

    assert count % size == 0
    lax.fori_loop(0, count // size, step, 0)


def every(level):
    return ((1, 26, 2), (1, 18, 3), (4, 32, 4), (1, 16, 8))[level]


def span(level, depth):
    if level >= 2:
        return HX[level], GRID[level][0], (8 if level == 2 else 16)
    own = GRID[level][0] // SHARDS
    lo, count = HX[level] - depth, own + 2 * depth
    if level == 0:
        return lo, -(-count // 4) * 4, 4
    return lo, count, count // 2


def fill_noise(level, out, keys, base):
    nx, ny, nz = GRID[level]
    y, z = yz_global(level)
    plane = y * nz + z
    lo, count, _ = every(level)

    def row(x):
        index = plane + x_global(level, x) * (ny * nz)
        return [(out, (i, x), gaussian_like(index, keys[base + i])) for i in range(4)]

    blocks(lo, count, 1, row)


def derive(level, kap, wx, wy, wz, a, noise):
    nx, ny, nz = GRID[level]
    y, z = yz_global(level)
    y_first, y_last, z_first, z_last = y == 0, y == ny - 1, z == 0, z == nz - 1
    lo, count, size = every(level)

    def row(x0):
        stores = []
        for x in [x0 + i for i in range(size)]:
            xg = x_global(level, x)
            up, vp, sp = wx[x], wy[x], wz[x]
            um = jnp.where(xg == 0, 0.0, wx[x - 1])
            vm = jnp.where(y_first, 0.0, pltpu.roll(vp, 1, 0))
            sm = jnp.where(z_first, 0.0, pltpu.roll(sp, 1, 1))
            diag = kap[x] + up + um + vp + vm + sp + sm
            if level in (1, 3):
                diag = jnp.where(diag > 0.0, diag, 1.0)
            inv = 1.0 / diag
            root = lax.rsqrt(diag)
            values = (jnp.where(xg == nx - 1, 0.0, up) * inv, um * inv, jnp.where(y_last, 0.0, vp) * inv, vm * inv,
                      jnp.where(z_last, 0.0, sp) * inv, sm * inv, diag, inv)
            stores += [(a, (i, x), v) for i, v in enumerate(values)]
            stores += [(noise, (i, x), noise[i, x] * root) for i in range(4)]
        return stores

    blocks(lo, count, size, row)


def scale_rhs(level, rhs, a):
    lo, count, size = every(level)
    blocks(lo, count, size, lambda x0: [(rhs, x0 + i, rhs[x0 + i] * a[7, x0 + i]) for i in range(size)])


def around(level, f, a, x0, size):
    s, w = S[level], W[level]
    v = [f[x0 + i] for i in range(-1, size + 1)]
    out = []
    for i in range(size):
        x, own = x0 + i, v[i + 1]
        t = a[0, x] * v[i + 2] + a[1, x] * v[i]
        u = a[2, x] * pltpu.roll(own, s - 1, 0) + a[3, x] * pltpu.roll(own, 1, 0)
        t = (t + u) + (a[4, x] * pltpu.roll(own, w - 1, 1) + a[5, x] * pltpu.roll(own, 1, 1))
        out.append((x, own, t))
    return out


def colored(level, x0, color):
    shape = (S[level], W[level])
    odd = (iota(shape, 0) + iota(shape, 1) + (x0 + (HX[level] + HY[level]))) & 1
    return odd == color, odd != color


def half_sweep(level, f, rhs, a, noise, sweep, color, depth):
    lo, count, size = span(level, depth)

    def rows(x0):
        masks = colored(level, x0, color)
        return [(f, x, jnp.where(masks[i % 2], rhs[x] + t + noise[sweep, x], own))
                for i, (x, own, t) in enumerate(around(level, f, a, x0, size))]

    blocks(lo, count, size, rows)


def first_half(level, f, rhs, noise, sweep, depth):
    lo, count, size = span(level, depth)

    def rows(x0):
        masks = colored(level, x0, 0)
        return [(f, x0 + i, jnp.where(masks[i % 2], rhs[x0 + i] + noise[sweep, x0 + i], 0.0)) for i in range(size)]

    blocks(lo, count, size, rows)


def sweeps(level, f, rhs, a, noise, leg, depth, from_zero=False):
    for i in range(4):
        if from_zero and i == 0:
            first_half(level, f, rhs, noise, 0, depth)
        else:
            half_sweep(level, f, rhs, a, noise, 2 * leg + i // 2, i % 2, depth - i)


def residual(level, f, rhs, a, out, y0, y1):
    lo, count, size = span(level, 0)
    size = min(size, 8)

    def rows(x0):
        return [(out, (x - lo, pl.ds(0, y1 - y0), slice(None)), (a[6, x] * (rhs[x] + t - v))[y0:y1, 0:128])
                for x, v, t in around(level, f, a, x0, size)]

    blocks(lo, count, size, rows)


def pairs(ref, cx, y0, n, xs=(0, 1), ys=(0, 1)):
    total = None
    for dx in xs:
        for dy in ys:
            v = ref[2 * cx + dx, pl.ds(y0 + dy, n, stride=2), :]
            total = v if total is None else total + v
    return total


def halve(rows, cols, start_r, limit, start_c, odd=False):
    r, c = iota((rows, cols), 0) - start_r, iota((rows, cols), 1) - start_c
    hit = (lax.shift_right_arithmetic(r, 1) == c) & (r >= 0) & (r < limit)
    if odd:
        hit = hit & (r & 1 == 1)
    return hit.astype(F32)


class Halo:
    def __init__(self, level, field, depth, packs, sems, tight=None):
        self.level, self.field, self.depth = level, field, depth
        self.send_up, self.send_down, self.got_up, self.got_down = packs
        self.ssem, self.rsem = sems
        self.tight = tight
        self.n = GRID[level][0] // SHARDS
        self.lanes = GRID[level][2] // SHARDS

    def plane_copies(self):
        n, d, hx, hy = self.n, self.depth, HX[self.level], HY[self.level]
        out = []
        moves = [(1, 0), (-1, 0), (0, 1), (0, -1), (1, 1), (1, -1), (-1, 1), (-1, -1)]
        for i, (mx, my) in enumerate(moves):
            sx, dx, lx = {0: (hx, hx, n), 1: (hx + n - d, hx - d, d), -1: (hx, hx + n, d)}[mx]
            sy, dy, ly = {0: (hy, hy, n), 1: (hy + n - 8, hy - 8, 8), -1: (hy, hy + n, 8)}[my]
            src = self.field.at[:, pl.ds(sx, lx), pl.ds(sy, ly), pl.ds(0, 128)]
            dst = self.field.at[:, pl.ds(dx, lx), pl.ds(dy, ly), pl.ds(0, 128)]
            if self.tight and my:
                sent, got, j = self.tight[:2] + (i - 2,) if i < 4 else self.tight[2:] + (i - 4,)
                src, dst = sent.at[j], got.at[j]
            out.append(pltpu.make_async_remote_copy(
                src_ref=src, dst_ref=dst,
                send_sem=self.ssem.at[i], recv_sem=self.rsem.at[i],
                device_id=neighbour(gx=mx, gy=my), device_id_type=MESH))
        return out

    def depth_copies(self):
        out = []
        for i, (mz, src, dst) in enumerate(((1, self.send_up, self.got_up), (-1, self.send_down, self.got_down))):
            out.append(pltpu.make_async_remote_copy(
                src_ref=src, dst_ref=dst, send_sem=self.ssem.at[8 + i], recv_sem=self.rsem.at[8 + i],
                device_id=neighbour(gz=mz), device_id_type=MESH))
        return out

    def plane_start(self):
        copies = self.plane_copies()
        if self.tight:
            for c in copies[:2]:
                c.start()
            self.stage(True)
            for c in copies[2:]:
                c.start()
        else:
            for c in copies:
                c.start()

    def stage(self, out):
        sent_y, got_y, sent_xy, got_xy = self.tight
        fields, hx = self.field.shape[0], HX[0]

        def face(x, c):
            for j in range(2):
                for f in range(fields):
                    rows = pl.ds(5 * f, 5)
                    if out:
                        sent_y[j, x, rows, :] = self.field[f, hx + x, pl.ds(8 if j else 19, 5), pl.ds(0, 128)]
                    else:
                        self.field[f, hx + x, pl.ds(24 if j else 3, 5), pl.ds(0, 128)] = got_y[j, x, rows, :]
            return c

        def corner(x, c):
            for j in range(4):
                for f in range(fields):
                    rows = pl.ds(4 * f, 4)
                    if out:
                        xs, ys = (6 if j >= 2 else 18), (8 if j % 2 else 20)
                        sent_xy[j, x, rows, :] = self.field[f, xs + x, pl.ds(ys, 4), pl.ds(0, 128)]
                    else:
                        xd, yd = (22 if j >= 2 else 2), (24 if j % 2 else 4)
                        self.field[f, xd + x, pl.ds(yd, 4), pl.ds(0, 128)] = got_xy[j, x, rows, :]
            return c

        lax.fori_loop(0, 16, face, 0)
        lax.fori_loop(0, 4, corner, 0)

    def plane_wait(self):
        for c in self.plane_copies():
            c.wait_recv()
        for c in self.plane_copies():
            c.wait_send()
        if self.tight:
            self.stage(False)

    def depth_start(self):
        st = S[self.level] // 8
        groups = X[self.level] // 4
        slot = lax.shift_right_logical(iota((8, 128), 1), 3)
        ahead = 15 if self.level == 0 else 7

        def pack(f, c):
            for g in range(groups):
                up = down = None
                for k in range(4 * st):
                    v = self.field[f, 4 * g + k // st, pl.ds(8 * (k % st), 8), pl.ds(0, 128)]
                    v = pltpu.roll(v, 8 * k, 1) if k else v
                    up = v if up is None else jnp.where(slot == (k + ahead) % 16, v, up)
                    down = v if down is None else jnp.where(slot == k, v, down)
                self.send_up[f, g] = up
                self.send_down[f, g] = down
            return c

        lax.fori_loop(0, self.field.shape[0], pack, 0)
        for c in self.depth_copies():
            c.start()

    def depth_wait(self):
        for c in self.depth_copies():
            c.wait_recv()
        for c in self.depth_copies():
            c.wait_send()
        st = S[self.level] // 8
        groups = X[self.level] // 4
        lane = iota((8, 128), 1)
        even = lax.shift_right_logical(lane, 3) & 1 == 0
        fine = self.level == 0
        at = 0 if fine else self.lanes

        def unpack(f, c):
            for g in range(groups):
                below, above = self.got_up[f, g], self.got_down[f, g]
                merged = (jnp.where(even, above, below), jnp.where(even, below, above))
                for k in range(4 * st):
                    rows = pl.ds(8 * (k % st), 8)
                    x = 4 * g + k // st
                    both = pltpu.roll(merged[k % 2], (at - 8 * k) % 128, 1)
                    if fine:
                        self.field[f, x, rows, pl.ds(128, 128)] = both
                    else:
                        own = self.field[f, x, rows, pl.ds(0, 128)]
                        self.field[f, x, rows, pl.ds(0, 128)] = jnp.where(lane < 64, own, both)
            return c

        lax.fori_loop(0, self.field.shape[0], unpack, 0)


class Gather:
    def __init__(self, by_x, by_xy, plane, below, above, sems):
        self.by_x, self.by_xy, self.plane, self.below, self.above = by_x, by_xy, plane, below, above
        self.ssem, self.rsem = sems

    def ring(self, axis, src, dst, base):
        out = []
        me = lax.axis_index(axis)
        for i, m in enumerate((1, 7, 2, 6, 3, 5, 4)):
            out.append(pltpu.make_async_remote_copy(
                src_ref=src, dst_ref=dst.at[me], send_sem=self.ssem.at[base + i], recv_sem=self.rsem.at[base + i],
                device_id={axis: lax.rem(me + m, SHARDS)}, device_id_type=MESH))
        return out

    def x_copies(self):
        return self.ring("gx", self.by_x.at[lax.axis_index("gx")], self.by_x, 0)

    def y_copies(self):
        return self.ring("gy", self.by_xy.at[lax.axis_index("gy")], self.by_xy, 7)

    def z_copies(self):
        return [
            pltpu.make_async_remote_copy(
                src_ref=self.plane, dst_ref=dst, send_sem=self.ssem.at[14 + i], recv_sem=self.rsem.at[14 + i],
                device_id=neighbour(gz=m), device_id_type=MESH)
            for i, (m, dst) in enumerate(((1, self.below), (-1, self.above)))]

    def wait(self, copies):
        for c in copies:
            c.wait_recv()
        for c in copies:
            c.wait_send()

    def x_start(self):
        for c in self.x_copies():
            c.start()

    def y_start(self):
        self.wait(self.x_copies())
        me = lax.axis_index("gy")
        for i in range(SHARDS):
            self.by_xy[me, i] = self.by_x[i]
        for c in self.y_copies():
            c.start()

    def z_start(self):
        self.wait(self.y_copies())

        def put(i, c):
            gx, gy = i // SHARDS, i % SHARDS
            for f in range(self.plane.shape[0]):
                self.plane[f, gx, pl.ds(4 * gy, 4), :] = self.by_xy[gy, gx, f]
            return c

        lax.fori_loop(0, SHARDS * SHARDS, put, 0)
        for c in self.z_copies():
            c.start()

    def finish(self, outs):
        self.wait(self.z_copies())
        lane = iota((32, 128), 1)

        def put(gx, c):
            for f, out in enumerate(outs):
                own, low, high = self.plane[f, gx], self.below[f, gx], self.above[f, gx]
                for xx in range(4):
                    v = jnp.where(lane < 32, pltpu.roll(low, (-32 * xx) % 128, 1),
                                  jnp.where(lane < 64, pltpu.roll(own, (32 - 32 * xx) % 128, 1),
                                            pltpu.roll(high, (64 - 32 * xx) % 128, 1)))
                    out[HX[2] + 4 * gx + xx] = v
            return c

        lax.fori_loop(0, SHARDS, put, 0)


def kernel(keys, state, data, kappa, weight_x, weight_y, weight_z, out,
           f0, xd0, a0, n0, c1, r1, f1, xd1, a1, n1, c2, r2, f2, a2, n2, c3, r3, f3, a3, n3,
           res, t64, t256,
           p0a, p0b, p0c, p0d, pxa, pxb, pxc, pxd, pca, pcb, pcc, pcd, pra, prb, prc, prd, pya, pyb, pyc, pyd,
           gcx, gcxy, gcp, gcl, gch, grx, grxy, grp, grl, grh,
           ysent, ygot, csent, cgot, ssem, rsem):
    def sems(i):
        return ssem.at[i], rsem.at[i]

    bar = pltpu.get_barrier_semaphore()

    for x in range(HX[2]):
        for at in (x, X[2] - 1 - x):
            f2[at] = jnp.zeros(f2.shape[1:], F32)
    for at in (0, X[3] - 1):
        f3[at] = jnp.zeros(f3.shape[1:], F32)

    for i, ref in enumerate((state, data, kappa, weight_x, weight_y, weight_z)):
        def load(x, c, i=i, ref=ref):
            f0[i, HX[0] + x, pl.ds(8, 16), pl.ds(0, 128)] = ref[x]
            return c
        lax.fori_loop(0, 16, load, 0)

    partners = [{"gx": m} for m in range(1, 8)] + [{"gy": m} for m in range(1, 8)] + [{"gz": 1}, {"gz": -1}]
    partners += [{"gx": a, "gy": b} for a in (1, -1) for b in (1, -1)]
    for p in partners:
        pl.semaphore_signal(bar, inc=1, device_id=neighbour(**p), device_id_type=MESH)
    pl.semaphore_wait(bar, len(partners))

    halo0 = Halo(0, f0, 5, (p0a, p0b, p0c, p0d), sems(0), (ysent, ygot, csent, cgot))
    halox0 = Halo(0, xd0, 4, (pxa, pxb, pxc, pxd), sems(1))
    haloc1 = Halo(1, c1, 6, (pca, pcb, pcc, pcd), sems(2))
    halor1 = Halo(1, r1, 6, (pra, prb, prc, prd), sems(3))
    halox1 = Halo(1, xd1, 6, (pya, pyb, pyc, pyd), sems(4))
    gatherc = Gather(gcx, gcxy, gcp, gcl, gch, sems(5))
    gatherr = Gather(grx, grxy, grp, grl, grh, sems(6))

    halo0.plane_start()

    m01, m01_odd = halve(128, 128, 0, 128, 0), halve(128, 128, 0, 128, 0, True)
    both, odd = (0, 1), (1,)
    for i, (ref, xs, ys, m) in enumerate(((kappa, both, both, m01), (weight_x, odd, both, m01),
                                          (weight_y, both, odd, m01), (weight_z, both, both, m01_odd))):
        for cx in range(8):
            t64[pl.ds(8 * cx, 8), :] = pairs(ref, cx, 0, 8, xs, ys)
        t = dot(t64[...], m)
        for cx in range(8):
            c1[i, HX[1] + cx, pl.ds(8, 8), :] = t[8 * cx:8 * cx + 8]
    gx = lax.axis_index("gx")
    for i, (xs, ys, flag) in enumerate(((both, both, False), (odd, both, False), (both, odd, False), (both, both, True))):
        t = jnp.zeros((4, 128), F32)
        for cx in range(4):
            t = t + dot(pairs(c1.at[i], 3 + cx, 8, 4, xs, ys), halve(128, 128, 0, 64, 32 * cx, flag))
        gcx[gx, i] = t

    fill_noise(0, n0, keys, 0)
    halo0.plane_wait()
    halo0.depth_start()
    gatherc.x_start()
    haloc1.plane_start()
    fill_noise(1, n1, keys, 4)
    halo0.depth_wait()
    gatherc.y_start()

    x0, b0 = f0.at[0], f0.at[1]
    derive(0, f0.at[2], f0.at[3], f0.at[4], f0.at[5], a0, n0)
    scale_rhs(0, b0, a0)
    sweeps(0, x0, b0, a0, n0, 0, 4)
    residual(0, x0, b0, a0, res, 8, 24)
    for cx in range(8):
        t64[pl.ds(8 * cx, 8), :] = pairs(res, cx, 0, 8)
    t = dot(t64[...], m01)
    for cx in range(8):
        r1[0, HX[1] + cx, pl.ds(8, 8), :] = t[8 * cx:8 * cx + 8]
    halor1.plane_start()

    def keep0(x, c):
        xd0[0, x, pl.ds(8, 16), pl.ds(0, 128)] = x0[x, pl.ds(8, 16), pl.ds(0, 128)]
        return c
    lax.fori_loop(HX[0], HX[0] + 16, keep0, 0)
    halox0.plane_start()
    haloc1.plane_wait()
    haloc1.depth_start()
    halor1.plane_wait()
    halor1.depth_start()
    haloc1.depth_wait()
    derive(1, c1.at[0], c1.at[1], c1.at[2], c1.at[3], a1, n1)
    gatherc.z_start()
    halox0.plane_wait()
    halox0.depth_start()
    halor1.depth_wait()

    b1 = r1.at[0]
    scale_rhs(1, b1, a1)
    sweeps(1, f1, b1, a1, n1, 0, 4, True)
    residual(1, f1, b1, a1, res, 8, 16)
    t = jnp.zeros((4, 128), F32)
    for cx in range(4):
        t = t + dot(pairs(res, cx, 0, 4), halve(128, 128, 0, 64, 32 * cx))
    grx[gx, 0] = t
    gatherr.x_start()

    def keep1(x, c):
        xd1[0, x, pl.ds(8, 8), :] = f1[x, pl.ds(8, 8), :]
        return c
    lax.fori_loop(HX[1], HX[1] + 8, keep1, 0)
    halox1.plane_start()
    fill_noise(2, n2, keys, 8)
    gatherc.finish([c2.at[i] for i in range(4)])
    derive(2, c2.at[0], c2.at[1], c2.at[2], c2.at[3], a2, n2)
    gatherr.y_start()
    halox1.plane_wait()
    halox1.depth_start()
    fill_noise(3, n3, keys, 12)
    m23, m23_odd = halve(128, 128, 0, 96, 0), halve(128, 128, 0, 96, 0, True)
    for i, (xs, ys, m) in enumerate(((both, both, m23), (odd, both, m23), (both, odd, m23), (both, both, m23_odd))):
        for cx in range(16):
            t256[pl.ds(16 * cx, 16), :] = pairs(c2.at[i], 2 + cx, 0, 16, xs, ys)
        t = dot(t256[...], m)
        for cx in range(16):
            c3[i, HX[3] + cx] = t[16 * cx:16 * cx + 16]
    derive(3, c3.at[0], c3.at[1], c3.at[2], c3.at[3], a3, n3)
    halox0.depth_wait()
    gatherr.z_start()
    halox1.depth_wait()
    gatherr.finish([r2])

    scale_rhs(2, r2, a2)
    sweeps(2, f2, r2, a2, n2, 0, 0, True)
    residual(2, f2, r2, a2, res, 0, 32)
    for cx in range(16):
        t256[pl.ds(16 * cx, 16), :] = pairs(res, cx, 0, 16)
    t = dot(t256[...], m23)
    for cx in range(16):
        r3[HX[3] + cx] = t[16 * cx:16 * cx + 16]
    scale_rhs(3, r3, a3)
    sweeps(3, f3, r3, a3, n3, 0, 0, True)
    sweeps(3, f3, r3, a3, n3, 1, 0)
    for cx in range(16):
        t256[pl.ds(16 * cx, 16), :] = f3[HX[3] + cx]
    i3, i2 = iota((128, 128), 0), iota((128, 128), 1)
    t = dot(t256[...], ((lax.shift_right_logical(i2, 1) == i3) & (i2 < 96)).astype(F32))
    for cx in range(16):
        for dx in both:
            for dy in both:
                rows = pl.ds(dy, 16, stride=2)
                x = HX[2] + 2 * cx + dx
                f2[x, rows, :] = f2[x, rows, :] + t[16 * cx:16 * cx + 16]
    sweeps(2, f2, r2, a2, n2, 1, 0)

    gy = lax.axis_index("gy")
    z1 = relative_z(1, (128, 128))
    m21 = ((i3 == lax.shift_right_arithmetic(z1, 1) + 32) & (z1 >= -6) & (z1 < 70)).astype(F32)
    for j in range(10):
        v = f2[HX[2] + 4 * gx + (j - 3)]
        t256[pl.ds(16 * j, 16), :] = pltpu.roll(v, lax.rem(36 - 4 * gy, 32), 0)[:16]
    t = dot(t256[...], m21)
    for j in range(10):
        for dx in both:
            for dy in both:
                rows = pl.ds(dy, 12, stride=2)
                x = 2 * j + dx
                xd1[0, x, rows, :] = xd1[0, x, rows, :] + t[16 * j:16 * j + 12]
    sweeps(1, xd1.at[0], b1, a1, n1, 1, 5)

    z0 = relative_z(0, (128, 256))
    hit = iota((128, 256), 0) == (lax.shift_right_arithmetic(z0, 1) & 127)
    m10 = (hit & (z0 >= -4) & (z0 < 132)).astype(F32)
    for j in range(12):
        t256[pl.ds(16 * j, 16), :] = xd1[0, 4 + j, pl.ds(4, 16), :]
    t = dot(t256[pl.ds(0, 192), :], m10)
    for j in range(12):
        for dy in both:
            rows = pl.ds(dy, 16, stride=2)
            res[j, rows, :] = t[16 * j:16 * j + 16, :128]
            res[16 + j, rows, :] = t[16 * j:16 * j + 16, 128:]

    def add(j, c):
        for dx in both:
            x = 2 + 2 * j + dx
            xd0[0, x, :, pl.ds(0, 128)] = xd0[0, x, :, pl.ds(0, 128)] + res[j]
            xd0[0, x, :, pl.ds(128, 128)] = xd0[0, x, :, pl.ds(128, 128)] + res[16 + j]
        return c
    lax.fori_loop(0, 12, add, 0)
    sweeps(0, xd0.at[0], b0, a0, n0, 1, 3)

    def give(x, c):
        out[x] = xd0[0, HX[0] + x, pl.ds(8, 16), pl.ds(0, 128)]
        return c
    lax.fori_loop(0, 16, give, 0)


def level_scratch(level, fields):
    shape = (X[level], S[level], W[level])
    return [pltpu.VMEM((n,) + shape if n else shape, F32) for n in fields]


def packs(level, n):
    return [pltpu.VMEM((n, X[level] // 4, 8, 128), F32)] * 4


def gathers(n):
    return [pltpu.VMEM((8, n, 4, 128), F32), pltpu.VMEM((8, 8, n, 4, 128), F32)] + [
        pltpu.VMEM((n, 8, 32, 128), F32)] * 3


def per_device(state, data_term, kappa, weight_x, weight_y, weight_z, noise_keys):
    scratch = (
        level_scratch(0, (6, 1, 8, 4)) + level_scratch(1, (4, 1, 0, 1, 8, 4))
        + level_scratch(2, (4, 0, 0, 8, 4)) + level_scratch(3, (4, 0, 0, 8, 4))
        + [pltpu.VMEM((32, 32, 128), F32), pltpu.VMEM((64, 128), F32), pltpu.VMEM((256, 128), F32)]
        + packs(0, 6) + packs(0, 1) + packs(1, 4) + packs(1, 1) + packs(1, 1)
        + gathers(4) + gathers(1)
        + [pltpu.VMEM((2, 16, 32, 128), F32)] * 2 + [pltpu.VMEM((4, 4, 24, 128), F32)] * 2
        + [pltpu.SemaphoreType.DMA((7, 16)), pltpu.SemaphoreType.DMA((7, 16))])
    return pl.pallas_call(
        kernel,
        out_shape=jax.ShapeDtypeStruct(state.shape, F32),
        in_specs=[pl.BlockSpec(memory_space=pltpu.SMEM)] + [pl.BlockSpec(memory_space=pltpu.VMEM)] * 6,
        out_specs=pl.BlockSpec(memory_space=pltpu.VMEM),
        scratch_shapes=scratch,
        compiler_params=pltpu.CompilerParams(
            collective_id=0, has_side_effects=True, vmem_limit_bytes=56 * 2**20),
    )(noise_keys.reshape(16), state, data_term, kappa, weight_x, weight_y, weight_z)


def solution(mesh):
    spec = P(*AXES)
    return jax.shard_map(
        per_device, mesh=mesh, in_specs=(spec,) * 6 + (P(),), out_specs=spec, check_vma=False)
```

```python
import functools
import math

import jax
import jax.numpy as jnp
from jax import lax
from jax.experimental import pallas as pl
from jax.experimental.pallas import tpu as pltpu
from jax.sharding import PartitionSpec as P

AXES = ("gx", "gy", "gz")
MESH = pl.DeviceIdType.MESH
F32 = jnp.float32
SHARDS = 8
GRID = ((128, 128, 1024), (64, 64, 512), (32, 32, 256), (16, 16, 128))
X = (28, 20, 40, 18)
S = (32, 24, 32, 16)
W = (256, 128, 128, 128)
HX = (6, 6, 4, 1)
HY = (8, 8, 0, 0)


def neighbour(**moves):
    return {a: lax.rem(lax.axis_index(a) + (m + SHARDS), SHARDS) for a, m in moves.items() if m}


def dot(a, b):
    return jnp.dot(a, b, precision=lax.Precision.HIGHEST, preferred_element_type=F32)


def iota(shape, dim):
    return lax.broadcasted_iota(jnp.int32, shape, dim)


def mixing(h):
    h = h ^ lax.shift_right_logical(h, jnp.int32(16))
    h = h * jnp.int32(-2048144789)
    h = h ^ lax.shift_right_logical(h, jnp.int32(13))
    h = h * jnp.int32(-1028477387)
    h = h ^ lax.shift_right_logical(h, jnp.int32(16))
    return h


def gaussian_like(index, key):
    first = mixing(index * jnp.int32(-1640531535) ^ key)
    second = mixing(first ^ jnp.int32(1759714724))
    steps = lax.shift_right_logical(first, jnp.int32(8)) + lax.shift_right_logical(second, jnp.int32(8))
    return steps.astype(F32) * (math.sqrt(6.0) / 16777216.0) - math.sqrt(6.0)


def relative_z(level, shape):
    lane = iota(shape, len(shape) - 1)
    if level == 0:
        return jnp.where(lane < 192, lane, lane - 256)
    if level == 1:
        return jnp.where(lane < 96, lane, lane - 128)
    return lane - (32 if level == 2 else 16)


def x_global(level, x):
    n = GRID[level][0]
    start = lax.axis_index("gx") * (n // SHARDS) if level < 2 else 0
    return (start + x - HX[level] + n) & (n - 1)


def yz_global(level):
    shape = (S[level], W[level])
    ny, nz = GRID[level][1:]
    start = lax.axis_index("gy") * (ny // SHARDS) if level < 2 else 0
    y = (iota(shape, 0) + (start - HY[level] + ny)) & (ny - 1)
    z = (relative_z(level, shape) + (lax.axis_index("gz") * (nz // SHARDS) + nz)) & (nz - 1)
    return y, z


def blocks(lo, count, size, body):
    def step(i, c):
        for ref, at, value in body(lo + i * size):
            ref[at] = value
        return c

    assert count % size == 0
    lax.fori_loop(0, count // size, step, 0)


def every(level):
    return ((1, 26, 2), (1, 18, 3), (4, 32, 4), (1, 16, 8))[level]


def span(level, depth):
    if level >= 2:
        return HX[level], GRID[level][0], (8 if level == 2 else 16)
    own = GRID[level][0] // SHARDS
    lo, count = HX[level] - depth, own + 2 * depth
    if level == 0:
        return lo, -(-count // 4) * 4, 4
    return lo, count, count // 2


def fill_noise(level, out, keys):
    nx, ny, nz = GRID[level]
    y, z = yz_global(level)
    plane = y * nz + z
    lo, count, _ = every(level)

    def row(x):
        index = plane + x_global(level, x) * (ny * nz)
        return [(out, (i, x), gaussian_like(index, keys[i // 2, i % 2, level])) for i in range(4)]

    blocks(lo, count, 1, row)


def derive(level, kap, wx, wy, wz, a, noise):
    nx, ny, nz = GRID[level]
    y, z = yz_global(level)
    y_first, y_last, z_first, z_last = y == 0, y == ny - 1, z == 0, z == nz - 1
    lo, count, size = every(level)

    def row(x0):
        stores = []
        for x in [x0 + i for i in range(size)]:
            xg = x_global(level, x)
            up, vp, sp = wx[x], wy[x], wz[x]
            um = jnp.where(xg == 0, 0.0, wx[x - 1])
            vm = jnp.where(y_first, 0.0, pltpu.roll(vp, 1, 0))
            sm = jnp.where(z_first, 0.0, pltpu.roll(sp, 1, 1))
            diag = kap[x] + up + um + vp + vm + sp + sm
            if level in (1, 3):
                diag = jnp.where(diag > 0.0, diag, 1.0)
            inv = 1.0 / diag
            root = lax.rsqrt(diag)
            values = (jnp.where(xg == nx - 1, 0.0, up) * inv, um * inv, jnp.where(y_last, 0.0, vp) * inv, vm * inv,
                      jnp.where(z_last, 0.0, sp) * inv, sm * inv, diag, inv)
            stores += [(a, (i, x), v) for i, v in enumerate(values)]
            stores += [(noise, (i, x), noise[i, x] * root) for i in range(4)]
        return stores

    blocks(lo, count, size, row)


def scale_rhs(level, rhs, a):
    lo, count, size = every(level)
    blocks(lo, count, size, lambda x0: [(rhs, x0 + i, rhs[x0 + i] * a[7, x0 + i]) for i in range(size)])


def around(level, f, a, x0, size):
    s, w = S[level], W[level]
    v = [f[x0 + i] for i in range(-1, size + 1)]
    out = []
    for i in range(size):
        x, own = x0 + i, v[i + 1]
        t = a[0, x] * v[i + 2] + a[1, x] * v[i]
        u = a[2, x] * pltpu.roll(own, s - 1, 0) + a[3, x] * pltpu.roll(own, 1, 0)
        t = (t + u) + (a[4, x] * pltpu.roll(own, w - 1, 1) + a[5, x] * pltpu.roll(own, 1, 1))
        out.append((x, own, t))
    return out


def around_own(f, a, x0, size):
    rows, lanes, lane = pl.ds(8, 16), pl.ds(0, 128), iota((16, 128), 1)
    v = [f[x0 + i, rows, lanes] for i in range(-1, size + 1)]
    out = []
    for i in range(size):
        x, own = x0 + i, v[i + 1]
        side = f[x, rows, pl.ds(128, 128)]
        t = a[0, x, rows, lanes] * v[i + 2] + a[1, x, rows, lanes] * v[i]
        u = a[2, x, rows, lanes] * f[x, pl.ds(9, 16), lanes] + a[3, x, rows, lanes] * f[x, pl.ds(7, 16), lanes]
        after = jnp.where(lane == 127, pltpu.roll(side, 127, 1), pltpu.roll(own, 127, 1))
        before = jnp.where(lane == 0, pltpu.roll(side, 1, 1), pltpu.roll(own, 1, 1))
        out.append((x, own, (t + u) + (a[4, x, rows, lanes] * after + a[5, x, rows, lanes] * before)))
    return out


def last_half(f, rhs, a, noise, sweep, out):
    rows, lanes = pl.ds(8, 16), pl.ds(0, 128)

    def block(x0):
        masks = colored(0, x0, 1, (16, 128))
        return [(out, x - HX[0], jnp.where(masks[i % 2], rhs[x, rows, lanes] + t + noise[sweep, x, rows, lanes], own))
                for i, (x, own, t) in enumerate(around_own(f, a, x0, 8))]

    blocks(HX[0], 16, 8, block)


def residual_own(f, rhs, a, out):
    rows, lanes = pl.ds(8, 16), pl.ds(0, 128)

    def block(x0):
        return [(out, (x - HX[0], pl.ds(0, 16), slice(None)), a[6, x, rows, lanes] * (rhs[x, rows, lanes] + t - v))
                for x, v, t in around_own(f, a, x0, 8)]

    blocks(HX[0], 16, 8, block)


def colored(level, x0, color, shape=None):
    shape = shape or (S[level], W[level])
    odd = (iota(shape, 0) + iota(shape, 1) + (x0 + (HX[level] + HY[level]))) & 1
    return odd == color, odd != color


def half_sweep(level, f, rhs, a, noise, sweep, color, depth):
    lo, count, size = span(level, depth)

    def rows(x0):
        masks = colored(level, x0, color)
        return [(f, x, jnp.where(masks[i % 2], rhs[x] + t + noise[sweep, x], own))
                for i, (x, own, t) in enumerate(around(level, f, a, x0, size))]

    blocks(lo, count, size, rows)


def first_half(level, f, rhs, noise, sweep, depth):
    lo, count, size = span(level, depth)

    def rows(x0):
        masks = colored(level, x0, 0)
        return [(f, x0 + i, jnp.where(masks[i % 2], rhs[x0 + i] + noise[sweep, x0 + i], 0.0)) for i in range(size)]

    blocks(lo, count, size, rows)


def sweeps(level, f, rhs, a, noise, leg, depth, from_zero=False, halves=4):
    for i in range(halves):
        if from_zero and i == 0:
            first_half(level, f, rhs, noise, 0, depth)
        else:
            half_sweep(level, f, rhs, a, noise, 2 * leg + i // 2, i % 2, depth - i)


def residual(level, f, rhs, a, out, y0, y1):
    lo, count, size = span(level, 0)
    size = min(size, 8)

    def rows(x0):
        return [(out, (x - lo, pl.ds(0, y1 - y0), slice(None)), (a[6, x] * (rhs[x] + t - v))[y0:y1, 0:128])
                for x, v, t in around(level, f, a, x0, size)]

    blocks(lo, count, size, rows)


def pairs(ref, cx, y0, n, xs=(0, 1), ys=(0, 1)):
    total = None
    for dx in xs:
        for dy in ys:
            v = ref[2 * cx + dx, pl.ds(y0 + dy, n, stride=2), :]
            total = v if total is None else total + v
    return total


def halve(rows, cols, start_r, limit, start_c, odd=False):
    r, c = iota((rows, cols), 0) - start_r, iota((rows, cols), 1) - start_c
    hit = (lax.shift_right_arithmetic(r, 1) == c) & (r >= 0) & (r < limit)
    if odd:
        hit = hit & (r & 1 == 1)
    return hit.astype(F32)


class Halo:
    def __init__(self, level, field, depth, packs, sems, tight=None):
        self.level, self.field, self.depth = level, field, depth
        self.send_up, self.send_down, self.got_up, self.got_down = packs
        self.ssem, self.rsem = sems
        self.tight = tight
        self.n = GRID[level][0] // SHARDS
        self.lanes = GRID[level][2] // SHARDS

    def plane_copies(self):
        n, d, hx, hy = self.n, self.depth, HX[self.level], HY[self.level]
        out = []
        moves = [(1, 0), (-1, 0), (0, 1), (0, -1), (1, 1), (1, -1), (-1, 1), (-1, -1)]
        for i, (mx, my) in enumerate(moves):
            sx, dx, lx = {0: (hx, hx, n), 1: (hx + n - d, hx - d, d), -1: (hx, hx + n, d)}[mx]
            sy, dy, ly = {0: (hy, hy, n), 1: (hy + n - 8, hy - 8, 8), -1: (hy, hy + n, 8)}[my]
            src = self.field.at[:, pl.ds(sx, lx), pl.ds(sy, ly), pl.ds(0, 128)]
            dst = self.field.at[:, pl.ds(dx, lx), pl.ds(dy, ly), pl.ds(0, 128)]
            if self.level == 1 and self.tight:
                src = self.tight[0].at[:, pl.ds(sx, lx), pl.ds(sy, ly), :]
                dst = self.tight[0].at[:, pl.ds(dx, lx), pl.ds(dy, ly), :]
            elif self.tight and my:
                sent, got, j = self.tight[:2] + (i - 2,) if i < 4 else self.tight[2:] + (i - 4,)
                src, dst = sent.at[j], got.at[j]
            out.append(pltpu.make_async_remote_copy(
                src_ref=src, dst_ref=dst,
                send_sem=self.ssem.at[i], recv_sem=self.rsem.at[i],
                device_id=neighbour(gx=mx, gy=my), device_id_type=MESH))
        return out

    def depth_copies(self):
        out = []
        for i, (mz, src, dst) in enumerate(((1, self.send_up, self.got_up), (-1, self.send_down, self.got_down))):
            out.append(pltpu.make_async_remote_copy(
                src_ref=src, dst_ref=dst, send_sem=self.ssem.at[8 + i], recv_sem=self.rsem.at[8 + i],
                device_id=neighbour(gz=mz), device_id_type=MESH))
        return out

    def plane_start(self):
        copies = self.plane_copies()
        if self.tight and self.level == 0:
            for c in copies[:2]:
                c.start()
            self.stage(True)
            for c in copies[2:]:
                c.start()
        else:
            for c in copies:
                c.start()

    def stage(self, out):
        sent_y, got_y, sent_xy, got_xy = self.tight
        fields, hx = self.field.shape[0], HX[0]

        def face(x, c):
            for j in range(2):
                for f in range(fields):
                    rows = pl.ds(5 * f, 5)
                    if out:
                        sent_y[j, x, rows, :] = self.field[f, hx + x, pl.ds(8 if j else 19, 5), pl.ds(0, 128)]
                    else:
                        self.field[f, hx + x, pl.ds(24 if j else 3, 5), pl.ds(0, 128)] = got_y[j, x, rows, :]
            return c

        def corner(x, c):
            for j in range(4):
                for f in range(fields):
                    rows = pl.ds(4 * f, 4)
                    if out:
                        xs, ys = (6 if j >= 2 else 18), (8 if j % 2 else 20)
                        sent_xy[j, x, rows, :] = self.field[f, xs + x, pl.ds(ys, 4), pl.ds(0, 128)]
                    else:
                        xd, yd = (22 if j >= 2 else 2), (24 if j % 2 else 4)
                        self.field[f, xd + x, pl.ds(yd, 4), pl.ds(0, 128)] = got_xy[j, x, rows, :]
            return c

        lax.fori_loop(0, 16, face, 0)
        lax.fori_loop(0, 4, corner, 0)

    def plane_wait(self):
        for c in self.plane_copies():
            c.wait_recv()
        for c in self.plane_copies():
            c.wait_send()
        if self.tight and self.level == 0:
            self.stage(False)
        elif self.tight:
            self.split()

    def split(self):
        both = self.tight[0]

        def rows(x0):
            return [(self.field, (2 * i + j, x), pltpu.roll(both[i, x], 64, 1) if j else both[i, x])
                    for x in (x0, x0 + 1) for i in range(2) for j in range(2)]

        blocks(0, X[1], 2, rows)

    def depth_start(self):
        st = S[self.level] // 8
        groups = X[self.level] // 4
        slot = lax.shift_right_logical(iota((8, 128), 1), 3)
        ahead = 15 if self.level == 0 else 7

        def pack(f, c):
            for g in range(groups):
                up = down = None
                for k in range(4 * st):
                    v = self.field[f, 4 * g + k // st, pl.ds(8 * (k % st), 8), pl.ds(0, 128)]
                    v = pltpu.roll(v, 8 * k, 1) if k else v
                    up = v if up is None else jnp.where(slot == (k + ahead) % 16, v, up)
                    down = v if down is None else jnp.where(slot == k, v, down)
                self.send_up[f, g] = up
                self.send_down[f, g] = down
            return c

        lax.fori_loop(0, self.field.shape[0], pack, 0)
        for c in self.depth_copies():
            c.start()

    def depth_wait(self):
        for c in self.depth_copies():
            c.wait_recv()
        for c in self.depth_copies():
            c.wait_send()
        st = S[self.level] // 8
        groups = X[self.level] // 4
        lane = iota((8, 128), 1)
        even = lax.shift_right_logical(lane, 3) & 1 == 0
        fine = self.level == 0
        at = 0 if fine else self.lanes

        def unpack(f, c):
            for g in range(groups):
                below, above = self.got_up[f, g], self.got_down[f, g]
                merged = (jnp.where(even, above, below), jnp.where(even, below, above))
                for k in range(4 * st):
                    rows = pl.ds(8 * (k % st), 8)
                    x = 4 * g + k // st
                    both = pltpu.roll(merged[k % 2], (at - 8 * k) % 128, 1)
                    if fine:
                        self.field[f, x, rows, pl.ds(128, 128)] = both
                    else:
                        own = self.field[f, x, rows, pl.ds(0, 128)]
                        self.field[f, x, rows, pl.ds(0, 128)] = jnp.where(lane < 64, own, both)
            return c

        lax.fori_loop(0, self.field.shape[0], unpack, 0)


class Gather:
    def __init__(self, by_x, by_xy, plane, below, above, sems, relay=False):
        self.by_x, self.by_xy, self.plane, self.below, self.above = by_x, by_xy, plane, below, above
        self.ssem, self.rsem = sems
        self.relay = relay

    def ring(self, axis, src, dst, base, far=True):
        out = []
        me = lax.axis_index(axis)
        for i, m in enumerate((4, 3, 5, 2, 6, 1, 7) if far else (2, 6, 1, 7)):
            out.append(pltpu.make_async_remote_copy(
                src_ref=src, dst_ref=dst.at[me], send_sem=self.ssem.at[base + i], recv_sem=self.rsem.at[base + i],
                device_id={axis: lax.rem(me + m, SHARDS)}, device_id_type=MESH))
        return out

    def x_copies(self):
        return self.ring("gx", self.by_x.at[lax.axis_index("gx")], self.by_x, 0)

    def y_copies(self, far=True):
        return self.ring("gy", self.by_xy.at[lax.axis_index("gy")], self.by_xy, 7, far)

    def y_near(self):
        return self.y_copies(False)

    def y_far(self):
        out = []
        me = lax.axis_index("gy")
        for i, (whose, to) in enumerate(((6, 1), (6, 2), (2, 7))):
            block = self.by_xy.at[lax.rem(me + whose, SHARDS)]
            out.append(pltpu.make_async_remote_copy(
                src_ref=block, dst_ref=block, send_sem=self.ssem.at[11 + i], recv_sem=self.rsem.at[11 + i],
                device_id={"gy": lax.rem(me + to, SHARDS)}, device_id_type=MESH))
        return out

    def z_copies(self):
        return [
            pltpu.make_async_remote_copy(
                src_ref=self.plane, dst_ref=dst, send_sem=self.ssem.at[14 + i], recv_sem=self.rsem.at[14 + i],
                device_id=neighbour(gz=m), device_id_type=MESH)
            for i, (m, dst) in enumerate(((1, self.below), (-1, self.above)))]

    def wait(self, copies):
        for c in copies:
            c.wait_recv()
        for c in copies:
            c.wait_send()

    def x_start(self):
        for c in self.x_copies():
            c.start()

    def y_start(self):
        self.wait(self.x_copies())
        me = lax.axis_index("gy")
        for i in range(SHARDS):
            self.by_xy[me, i] = self.by_x[i]
        for c in self.y_near() if self.relay else self.y_copies():
            c.start()

    def y_more(self):
        self.wait(self.y_near())
        for c in self.y_far():
            c.start()

    def z_start(self):
        self.wait(self.y_far() if self.relay else self.y_copies())

        def put(i, c):
            gx, gy = i // SHARDS, i % SHARDS
            for f in range(self.plane.shape[0]):
                self.plane[f, gx, pl.ds(4 * gy, 4), :] = self.by_xy[gy, gx, f]
            return c

        lax.fori_loop(0, SHARDS * SHARDS, put, 0)
        for c in self.z_copies():
            c.start()

    def finish(self, outs):
        self.wait(self.z_copies())
        lane = iota((32, 128), 1)

        def put(gx, c):
            for f, out in enumerate(outs):
                own, low, high = self.plane[f, gx], self.below[f, gx], self.above[f, gx]
                for xx in range(4):
                    v = jnp.where(lane < 32, pltpu.roll(low, (-32 * xx) % 128, 1),
                                  jnp.where(lane < 64, pltpu.roll(own, (32 - 32 * xx) % 128, 1),
                                            pltpu.roll(high, (64 - 32 * xx) % 128, 1)))
                    out[HX[2] + 4 * gx + xx] = v
            return c

        lax.fori_loop(0, SHARDS, put, 0)


def kernel(keys, state, data, kappa, weight_x, weight_y, weight_z, out,
           f0, xd0, a0, n0, c1p, c1, r1, f1, xd1, a1, n1, c2, r2, f2, a2, n2, c3, r3, f3, a3, n3,
           res, t64, t256,
           p0a, p0b, p0c, p0d, pxa, pxb, pxc, pxd, pca, pcb, pcc, pcd, pra, prb, prc, prd, pya, pyb, pyc, pyd,
           gcx, gcxy, gcp, gcl, gch, grx, grxy, grp, grl, grh,
           ysent, ygot, csent, cgot, ssem, rsem):
    def sems(i):
        return ssem.at[i], rsem.at[i]

    bar = pltpu.get_barrier_semaphore()
    partners = [{"gx": m} for m in range(1, 8)] + [{"gy": m} for m in range(1, 8)] + [{"gz": 1}, {"gz": -1}]
    partners += [{"gx": a, "gy": b} for a in (1, -1) for b in (1, -1)]
    for p in partners:
        pl.semaphore_signal(bar, inc=1, device_id=neighbour(**p), device_id_type=MESH)

    for x in range(HX[2]):
        for at in (x, X[2] - 1 - x):
            f2[at] = jnp.zeros(f2.shape[1:], F32)
    for at in (0, X[3] - 1):
        f3[at] = jnp.zeros(f3.shape[1:], F32)

    for i, ref in enumerate((state, data, kappa, weight_x, weight_y, weight_z)):
        def load(x, c, i=i, ref=ref):
            f0[i, HX[0] + x, pl.ds(8, 16), pl.ds(0, 128)] = ref[x]
            return c
        lax.fori_loop(0, 16, load, 0)

    pl.semaphore_wait(bar, len(partners))

    halo0 = Halo(0, f0, 5, (p0a, p0b, p0c, p0d), sems(0), (ysent, ygot, csent, cgot))
    halox0 = Halo(0, xd0, 4, (pxa, pxb, pxc, pxd), sems(1))
    haloc1 = Halo(1, c1, 6, (pca, pcb, pcc, pcd), sems(2), (c1p,))
    halor1 = Halo(1, r1, 6, (pra, prb, prc, prd), sems(3))
    halox1 = Halo(1, xd1, 6, (pya, pyb, pyc, pyd), sems(4))
    gatherc = Gather(gcx, gcxy, gcp, gcl, gch, sems(5), True)
    gatherr = Gather(grx, grxy, grp, grl, grh, sems(6))

    halo0.plane_start()

    m01, m01_odd = halve(128, 128, 0, 128, 0), halve(128, 128, 0, 128, 0, True)
    both, odd = (0, 1), (1,)
    for i, (ref, xs, ys, m) in enumerate(((kappa, both, both, m01), (weight_x, odd, both, m01),
                                          (weight_y, both, odd, m01), (weight_z, both, both, m01_odd))):
        for cx in range(8):
            t64[pl.ds(8 * cx, 8), :] = pairs(ref, cx, 0, 8, xs, ys)
        t = dot(t64[...], m)
        for cx in range(8):
            c1[i, HX[1] + cx, pl.ds(8, 8), :] = t[8 * cx:8 * cx + 8]
            if i % 2:
                c1p[i // 2, HX[1] + cx, pl.ds(8, 8), :] = first[8 * cx:8 * cx + 8] + pltpu.roll(t, 64, 1)[8 * cx:8 * cx + 8]
        first = t
    gx = lax.axis_index("gx")
    for i, (xs, ys, flag) in enumerate(((both, both, False), (odd, both, False), (both, odd, False), (both, both, True))):
        t = jnp.zeros((4, 128), F32)
        for cx in range(4):
            t = t + dot(pairs(c1.at[i], 3 + cx, 8, 4, xs, ys), halve(128, 128, 0, 64, 32 * cx, flag))
        gcx[gx, i] = t

    fill_noise(0, n0, keys)
    halo0.plane_wait()
    halo0.depth_start()
    gatherc.x_start()
    haloc1.plane_start()
    fill_noise(1, n1, keys)
    fill_noise(2, n2, keys)
    fill_noise(3, n3, keys)
    halo0.depth_wait()
    gatherc.y_start()

    x0, b0 = f0.at[0], f0.at[1]
    derive(0, f0.at[2], f0.at[3], f0.at[4], f0.at[5], a0, n0)
    scale_rhs(0, b0, a0)
    sweeps(0, x0, b0, a0, n0, 0, 4)
    gatherc.y_more()
    residual_own(x0, b0, a0, res)
    for cx in range(8):
        t64[pl.ds(8 * cx, 8), :] = pairs(res, cx, 0, 8)
    t = dot(t64[...], m01)
    for cx in range(8):
        r1[0, HX[1] + cx, pl.ds(8, 8), :] = t[8 * cx:8 * cx + 8]
    halor1.plane_start()

    def keep0(x, c):
        xd0[0, x, pl.ds(8, 16), pl.ds(0, 128)] = x0[x, pl.ds(8, 16), pl.ds(0, 128)]
        return c
    lax.fori_loop(HX[0], HX[0] + 16, keep0, 0)
    haloc1.plane_wait()
    haloc1.depth_start()
    halor1.plane_wait()
    halor1.depth_start()
    halox0.plane_start()
    gatherc.z_start()
    haloc1.depth_wait()
    derive(1, c1.at[0], c1.at[1], c1.at[2], c1.at[3], a1, n1)
    halor1.depth_wait()

    b1 = r1.at[0]
    scale_rhs(1, b1, a1)
    sweeps(1, f1, b1, a1, n1, 0, 4, True)
    residual(1, f1, b1, a1, res, 8, 16)
    t = jnp.zeros((4, 128), F32)
    for cx in range(4):
        t = t + dot(pairs(res, cx, 0, 4), halve(128, 128, 0, 64, 32 * cx))
    grx[gx, 0] = t
    gatherr.x_start()

    def keep1(x, c):
        xd1[0, x, pl.ds(8, 8), :] = f1[x, pl.ds(8, 8), :]
        return c
    lax.fori_loop(HX[1], HX[1] + 8, keep1, 0)
    halox1.plane_start()
    halox0.plane_wait()
    halox0.depth_start()
    gatherr.y_start()
    gatherc.finish([c2.at[i] for i in range(4)])
    derive(2, c2.at[0], c2.at[1], c2.at[2], c2.at[3], a2, n2)
    halox1.plane_wait()
    halox1.depth_start()
    gatherr.z_start()
    m23, m23_odd = halve(128, 128, 0, 96, 0), halve(128, 128, 0, 96, 0, True)
    for i, (xs, ys, m) in enumerate(((both, both, m23), (odd, both, m23), (both, odd, m23), (both, both, m23_odd))):
        for cx in range(16):
            t256[pl.ds(16 * cx, 16), :] = pairs(c2.at[i], 2 + cx, 0, 16, xs, ys)
        t = dot(t256[...], m)
        for cx in range(16):
            c3[i, HX[3] + cx] = t[16 * cx:16 * cx + 16]
    derive(3, c3.at[0], c3.at[1], c3.at[2], c3.at[3], a3, n3)
    halox0.depth_wait()
    halox1.depth_wait()
    gatherr.finish([r2])

    scale_rhs(2, r2, a2)
    sweeps(2, f2, r2, a2, n2, 0, 0, True)
    residual(2, f2, r2, a2, res, 0, 32)
    for cx in range(16):
        t256[pl.ds(16 * cx, 16), :] = pairs(res, cx, 0, 16)
    t = dot(t256[...], m23)
    for cx in range(16):
        r3[HX[3] + cx] = t[16 * cx:16 * cx + 16]
    scale_rhs(3, r3, a3)
    sweeps(3, f3, r3, a3, n3, 0, 0, True)
    sweeps(3, f3, r3, a3, n3, 1, 0)
    for cx in range(16):
        t256[pl.ds(16 * cx, 16), :] = f3[HX[3] + cx]
    i3, i2 = iota((128, 128), 0), iota((128, 128), 1)
    t = dot(t256[...], ((lax.shift_right_logical(i2, 1) == i3) & (i2 < 96)).astype(F32))
    for cx in range(16):
        for dx in both:
            for dy in both:
                rows = pl.ds(dy, 16, stride=2)
                x = HX[2] + 2 * cx + dx
                f2[x, rows, :] = f2[x, rows, :] + t[16 * cx:16 * cx + 16]
    sweeps(2, f2, r2, a2, n2, 1, 0)

    gy = lax.axis_index("gy")
    z1 = relative_z(1, (128, 128))
    m21 = ((i3 == lax.shift_right_arithmetic(z1, 1) + 32) & (z1 >= -6) & (z1 < 70)).astype(F32)
    for j in range(10):
        v = f2[HX[2] + 4 * gx + (j - 3)]
        t256[pl.ds(16 * j, 16), :] = pltpu.roll(v, lax.rem(36 - 4 * gy, 32), 0)[:16]
    t = dot(t256[...], m21)
    for j in range(10):
        for dx in both:
            for dy in both:
                rows = pl.ds(dy, 12, stride=2)
                x = 2 * j + dx
                xd1[0, x, rows, :] = xd1[0, x, rows, :] + t[16 * j:16 * j + 12]
    sweeps(1, xd1.at[0], b1, a1, n1, 1, 5)

    z0 = relative_z(0, (128, 256))
    hit = iota((128, 256), 0) == (lax.shift_right_arithmetic(z0, 1) & 127)
    m10 = (hit & (z0 >= -4) & (z0 < 132)).astype(F32)
    for j in range(12):
        t256[pl.ds(16 * j, 16), :] = xd1[0, 4 + j, pl.ds(4, 16), :]
    t = dot(t256[pl.ds(0, 192), :], m10)
    for j in range(12):
        for dy in both:
            rows = pl.ds(dy, 16, stride=2)
            res[j, rows, :] = t[16 * j:16 * j + 16, :128]
            res[16 + j, rows, :] = t[16 * j:16 * j + 16, 128:]

    def add(j, c):
        for dx in both:
            x = 2 + 2 * j + dx
            xd0[0, x, :, pl.ds(0, 128)] = xd0[0, x, :, pl.ds(0, 128)] + res[j]
            xd0[0, x, :, pl.ds(128, 128)] = xd0[0, x, :, pl.ds(128, 128)] + res[16 + j]
        return c
    lax.fori_loop(0, 12, add, 0)
    sweeps(0, xd0.at[0], b0, a0, n0, 1, 3, halves=3)
    last_half(xd0.at[0], b0, a0, n0, 3, out)


def level_scratch(level, fields):
    shape = (X[level], S[level], W[level])
    return [pltpu.VMEM((n,) + shape if n else shape, F32) for n in fields]


def packs(level, n):
    return [pltpu.VMEM((n, X[level] // 4, 8, 128), F32)] * 4


def gathers(n):
    return [pltpu.VMEM((8, n, 4, 128), F32), pltpu.VMEM((8, 8, n, 4, 128), F32)] + [
        pltpu.VMEM((n, 8, 32, 128), F32)] * 3


def per_device(state, data_term, kappa, weight_x, weight_y, weight_z, noise_keys):
    scratch = (
        level_scratch(0, (6, 1, 8, 4)) + level_scratch(1, (2, 4, 1, 0, 1, 8, 4))
        + level_scratch(2, (4, 0, 0, 8, 4)) + level_scratch(3, (4, 0, 0, 8, 4))
        + [pltpu.VMEM((32, 32, 128), F32), pltpu.VMEM((64, 128), F32), pltpu.VMEM((256, 128), F32)]
        + packs(0, 6) + packs(0, 1) + packs(1, 4) + packs(1, 1) + packs(1, 1)
        + gathers(4) + gathers(1)
        + [pltpu.VMEM((2, 16, 32, 128), F32)] * 2 + [pltpu.VMEM((4, 4, 24, 128), F32)] * 2
        + [pltpu.SemaphoreType.DMA((7, 16)), pltpu.SemaphoreType.DMA((7, 16))])
    return pl.pallas_call(
        kernel,
        out_shape=jax.ShapeDtypeStruct(state.shape, F32),
        in_specs=[pl.BlockSpec(memory_space=pltpu.SMEM)] + [pl.BlockSpec(memory_space=pltpu.VMEM)] * 6,
        out_specs=pl.BlockSpec(memory_space=pltpu.VMEM),
        scratch_shapes=scratch,
        compiler_params=pltpu.CompilerParams(
            collective_id=0, has_side_effects=True, vmem_limit_bytes=56 * 2**20),
    )(noise_keys.transpose(1, 2, 0), state, data_term, kappa, weight_x, weight_y, weight_z)


def solution(mesh):
    spec = P(*AXES)
    return jax.shard_map(
        per_device, mesh=mesh, in_specs=(spec,) * 6 + (P(),), out_specs=spec, check_vma=False)
```

```python
import functools
import math

import jax
import jax.numpy as jnp
from jax import lax
from jax.experimental import pallas as pl
from jax.experimental.pallas import tpu as pltpu
from jax.sharding import PartitionSpec as P

AXES = ("gx", "gy", "gz")
MESH = pl.DeviceIdType.MESH
F32 = jnp.float32
SHARDS = 8
GRID = ((128, 128, 1024), (64, 64, 512), (32, 32, 256), (16, 16, 128))
X = (28, 20, 40, 18)
S = (32, 24, 32, 16)
W = (256, 128, 128, 128)
HX = (6, 6, 4, 1)
HY = (8, 8, 0, 0)


def neighbour(**moves):
    return {a: lax.rem(lax.axis_index(a) + (m + SHARDS), SHARDS) for a, m in moves.items() if m}


def dot(a, b):
    return jnp.dot(a, b, precision=lax.Precision.HIGHEST, preferred_element_type=F32)


def iota(shape, dim):
    return lax.broadcasted_iota(jnp.int32, shape, dim)


def mixing(h):
    h = h ^ lax.shift_right_logical(h, jnp.int32(16))
    h = h * jnp.int32(-2048144789)
    h = h ^ lax.shift_right_logical(h, jnp.int32(13))
    h = h * jnp.int32(-1028477387)
    h = h ^ lax.shift_right_logical(h, jnp.int32(16))
    return h


def gaussian_like(index, key):
    first = mixing(index * jnp.int32(-1640531535) ^ key)
    second = mixing(first ^ jnp.int32(1759714724))
    steps = lax.shift_right_logical(first, jnp.int32(8)) + lax.shift_right_logical(second, jnp.int32(8))
    return steps.astype(F32) * (math.sqrt(6.0) / 16777216.0) - math.sqrt(6.0)


def relative_z(level, shape):
    lane = iota(shape, len(shape) - 1)
    if level == 0:
        return jnp.where(lane < 192, lane, lane - 256)
    if level == 1:
        return jnp.where(lane < 96, lane, lane - 128)
    return lane - (32 if level == 2 else 16)


def x_global(level, x):
    n = GRID[level][0]
    start = lax.axis_index("gx") * (n // SHARDS) if level < 2 else 0
    return (start + x - HX[level] + n) & (n - 1)


def yz_global(level):
    shape = (S[level], W[level])
    ny, nz = GRID[level][1:]
    start = lax.axis_index("gy") * (ny // SHARDS) if level < 2 else 0
    y = (iota(shape, 0) + (start - HY[level] + ny)) & (ny - 1)
    z = (relative_z(level, shape) + (lax.axis_index("gz") * (nz // SHARDS) + nz)) & (nz - 1)
    return y, z


def blocks(lo, count, size, body):
    def step(i, c):
        for ref, at, value in body(lo + i * size):
            ref[at] = value
        return c

    assert count % size == 0
    lax.fori_loop(0, count // size, step, 0)


def every(level):
    return ((1, 26, 2), (1, 18, 3), (4, 32, 4), (1, 16, 8))[level]


def span(level, depth):
    if level >= 2:
        return HX[level], GRID[level][0], 16
    own = GRID[level][0] // SHARDS
    lo, count = HX[level] - depth, own + 2 * depth
    if level == 0:
        return (lo, 24, 8) if depth >= 3 else (lo, 20, 10)
    return lo, count, count


def fill_noise(level, out, keys):
    nx, ny, nz = GRID[level]
    y, z = yz_global(level)
    plane = y * nz + z
    lo, count, _ = every(level)

    def row(x):
        index = plane + x_global(level, x) * (ny * nz)
        return [(out, (i, x), gaussian_like(index, keys[i // 2, i % 2, level])) for i in range(4)]

    blocks(lo, count, 1, row)


def derive(level, kap, wx, wy, wz, a, noise, rhs=None):
    nx, ny, nz = GRID[level]
    y, z = yz_global(level)
    y_first, y_last, z_first, z_last = y == 0, y == ny - 1, z == 0, z == nz - 1
    lo, count, size = every(level)

    def row(x0):
        stores = []
        for x in [x0 + i for i in range(size)]:
            xg = x_global(level, x)
            up, vp, sp = wx[x], wy[x], wz[x]
            um = jnp.where(xg == 0, 0.0, wx[x - 1])
            vm = jnp.where(y_first, 0.0, pltpu.roll(vp, 1, 0))
            sm = jnp.where(z_first, 0.0, pltpu.roll(sp, 1, 1))
            diag = kap[x] + up + um + vp + vm + sp + sm
            if level in (1, 3):
                diag = jnp.where(diag > 0.0, diag, 1.0)
            inv = 1.0 / diag
            root = lax.rsqrt(diag)
            values = (jnp.where(xg == nx - 1, 0.0, up) * inv, um * inv, jnp.where(y_last, 0.0, vp) * inv, vm * inv,
                      jnp.where(z_last, 0.0, sp) * inv, sm * inv, diag, inv)
            stores += [(a, (i, x), v) for i, v in enumerate(values)]
            stores += [(noise, (i, x), noise[i, x] * root) for i in range(4)]
            if rhs is not None:
                stores.append((rhs, x, rhs[x] * inv))
        return stores

    blocks(lo, count, size, row)


def scale_rhs(level, rhs, a):
    lo, count, size = every(level)
    blocks(lo, count, size, lambda x0: [(rhs, x0 + i, rhs[x0 + i] * a[7, x0 + i]) for i in range(size)])


def around(level, f, a, x0, size):
    s, w = S[level], W[level]
    v = [f[x0 + i] for i in range(-1, size + 1)]
    out = []
    for i in range(size):
        x, own = x0 + i, v[i + 1]
        t = a[0, x] * v[i + 2] + a[1, x] * v[i]
        u = a[2, x] * pltpu.roll(own, s - 1, 0) + a[3, x] * pltpu.roll(own, 1, 0)
        t = (t + u) + (a[4, x] * pltpu.roll(own, w - 1, 1) + a[5, x] * pltpu.roll(own, 1, 1))
        out.append((x, own, t))
    return out


def around_own(f, a, x0, size):
    rows, lanes, lane = pl.ds(8, 16), pl.ds(0, 128), iota((16, 128), 1)
    v = [f[x0 + i, rows, lanes] for i in range(-1, size + 1)]
    out = []
    for i in range(size):
        x, own = x0 + i, v[i + 1]
        side = f[x, rows, pl.ds(128, 128)]
        t = a[0, x, rows, lanes] * v[i + 2] + a[1, x, rows, lanes] * v[i]
        u = a[2, x, rows, lanes] * f[x, pl.ds(9, 16), lanes] + a[3, x, rows, lanes] * f[x, pl.ds(7, 16), lanes]
        after = jnp.where(lane == 127, pltpu.roll(side, 127, 1), pltpu.roll(own, 127, 1))
        before = jnp.where(lane == 0, pltpu.roll(side, 1, 1), pltpu.roll(own, 1, 1))
        out.append((x, own, (t + u) + (a[4, x, rows, lanes] * after + a[5, x, rows, lanes] * before)))
    return out


def last_half(f, rhs, a, noise, sweep, out):
    rows, lanes = pl.ds(8, 16), pl.ds(0, 128)

    def block(x0):
        masks = colored(0, x0, 1, (16, 128))
        return [(out, x - HX[0], jnp.where(masks[i % 2], rhs[x, rows, lanes] + t + noise[sweep, x, rows, lanes], own))
                for i, (x, own, t) in enumerate(around_own(f, a, x0, 8))]

    blocks(HX[0], 16, 8, block)


def residual_own(f, rhs, a, out):
    rows, lanes = pl.ds(8, 16), pl.ds(0, 128)

    def block(x0):
        return [(out, (x - HX[0], pl.ds(0, 16), slice(None)), a[6, x, rows, lanes] * (rhs[x, rows, lanes] + t - v))
                for x, v, t in around_own(f, a, x0, 8)]

    blocks(HX[0], 16, 8, block)


def colored(level, x0, color, shape=None):
    shape = shape or (S[level], W[level])
    odd = (iota(shape, 0) + iota(shape, 1) + (x0 + (HX[level] + HY[level]))) & 1
    return odd == color, odd != color


def half_sweep(level, f, rhs, a, noise, sweep, color, depth):
    lo, count, size = span(level, depth)

    def rows(x0):
        masks = colored(level, x0, color)
        return [(f, x, jnp.where(masks[i % 2], rhs[x] + t + noise[sweep, x], own))
                for i, (x, own, t) in enumerate(around(level, f, a, x0, size))]

    blocks(lo, count, size, rows)


def first_half(level, f, rhs, noise, sweep, depth):
    lo, count, size = span(level, depth)

    def rows(x0):
        masks = colored(level, x0, 0)
        return [(f, x0 + i, jnp.where(masks[i % 2], rhs[x0 + i] + noise[sweep, x0 + i], 0.0)) for i in range(size)]

    blocks(lo, count, size, rows)


def sweeps(level, f, rhs, a, noise, leg, depth, from_zero=False, halves=4):
    for i in range(halves):
        if from_zero and i == 0:
            first_half(level, f, rhs, noise, 0, depth)
        else:
            half_sweep(level, f, rhs, a, noise, 2 * leg + i // 2, i % 2, depth - i)


def residual(level, f, rhs, a, out, y0, y1):
    lo, count, size = span(level, 0)
    size = min(size, 8)

    def rows(x0):
        return [(out, (x - lo, pl.ds(0, y1 - y0), slice(None)), (a[6, x] * (rhs[x] + t - v))[y0:y1, 0:128])
                for x, v, t in around(level, f, a, x0, size)]

    blocks(lo, count, size, rows)


def pairs(ref, cx, y0, n, xs=(0, 1), ys=(0, 1)):
    total = None
    for dx in xs:
        for dy in ys:
            v = ref[2 * cx + dx, pl.ds(y0 + dy, n, stride=2), :]
            total = v if total is None else total + v
    return total


def halve(rows, cols, start_r, limit, start_c, odd=False):
    r, c = iota((rows, cols), 0) - start_r, iota((rows, cols), 1) - start_c
    hit = (lax.shift_right_arithmetic(r, 1) == c) & (r >= 0) & (r < limit)
    if odd:
        hit = hit & (r & 1 == 1)
    return hit.astype(F32)


class Halo:
    def __init__(self, level, field, depth, packs, sems, tight=None):
        self.level, self.field, self.depth = level, field, depth
        self.send_up, self.send_down, self.got_up, self.got_down = packs
        self.ssem, self.rsem = sems
        self.tight = tight
        self.n = GRID[level][0] // SHARDS
        self.lanes = GRID[level][2] // SHARDS

    def plane_copies(self):
        n, d, hx, hy = self.n, self.depth, HX[self.level], HY[self.level]
        out = []
        moves = [(1, 0), (-1, 0), (0, 1), (0, -1), (1, 1), (1, -1), (-1, 1), (-1, -1)]
        for i, (mx, my) in enumerate(moves):
            sx, dx, lx = {0: (hx, hx, n), 1: (hx + n - d, hx - d, d), -1: (hx, hx + n, d)}[mx]
            sy, dy, ly = {0: (hy, hy, n), 1: (hy + n - 8, hy - 8, 8), -1: (hy, hy + n, 8)}[my]
            src = self.field.at[:, pl.ds(sx, lx), pl.ds(sy, ly), pl.ds(0, 128)]
            dst = self.field.at[:, pl.ds(dx, lx), pl.ds(dy, ly), pl.ds(0, 128)]
            if self.level == 1 and self.tight:
                src = self.tight[0].at[:, pl.ds(sx, lx), pl.ds(sy, ly), :]
                dst = self.tight[0].at[:, pl.ds(dx, lx), pl.ds(dy, ly), :]
            elif self.tight and my:
                sent, got, j = self.tight[:2] + (i - 2,) if i < 4 else self.tight[2:] + (i - 4,)
                src, dst = sent.at[j], got.at[j]
            out.append(pltpu.make_async_remote_copy(
                src_ref=src, dst_ref=dst,
                send_sem=self.ssem.at[i], recv_sem=self.rsem.at[i],
                device_id=neighbour(gx=mx, gy=my), device_id_type=MESH))
        return out

    def depth_copies(self):
        out = []
        for i, (mz, src, dst) in enumerate(((1, self.send_up, self.got_up), (-1, self.send_down, self.got_down))):
            out.append(pltpu.make_async_remote_copy(
                src_ref=src, dst_ref=dst, send_sem=self.ssem.at[8 + i], recv_sem=self.rsem.at[8 + i],
                device_id=neighbour(gz=mz), device_id_type=MESH))
        return out

    def plane_start(self):
        copies = self.plane_copies()
        if self.tight and self.level == 0:
            for c in copies[:2]:
                c.start()
            self.stage(True)
            for c in copies[2:]:
                c.start()
        else:
            for c in copies:
                c.start()

    def stage(self, out):
        sent_y, got_y, sent_xy, got_xy = self.tight
        fields, hx = self.field.shape[0], HX[0]

        def face(x, c):
            for j in range(2):
                for f in range(fields):
                    rows = pl.ds(5 * f, 5)
                    if out:
                        sent_y[j, x, rows, :] = self.field[f, hx + x, pl.ds(8 if j else 19, 5), pl.ds(0, 128)]
                    else:
                        self.field[f, hx + x, pl.ds(24 if j else 3, 5), pl.ds(0, 128)] = got_y[j, x, rows, :]
            return c

        def corner(j):
            at = 0
            for i in range(4):
                n = 4 - i
                xs, xd = (6 + i, 22 + i) if j >= 2 else (21 - i, 5 - i)
                ys, yd = (8, 24) if j % 2 else (24 - n, 8 - n)
                for f in range(fields):
                    rows = pl.ds(at, n)
                    if out:
                        sent_xy[j, rows, :] = self.field[f, xs, pl.ds(ys, n), pl.ds(0, 128)]
                    else:
                        self.field[f, xd, pl.ds(yd, n), pl.ds(0, 128)] = got_xy[j, rows, :]
                    at += n

        lax.fori_loop(0, 16, face, 0)
        for j in range(4):
            corner(j)

    def plane_wait(self):
        for c in self.plane_copies():
            c.wait_recv()
        for c in self.plane_copies():
            c.wait_send()
        if self.tight and self.level == 0:
            self.stage(False)
        elif self.tight:
            self.split()

    def split(self):
        both = self.tight[0]

        def rows(x0):
            return [(self.field, (2 * i + j, x), pltpu.roll(both[i, x], 64, 1) if j else both[i, x])
                    for x in (x0, x0 + 1) for i in range(2) for j in range(2)]

        blocks(0, X[1], 2, rows)

    def depth_start(self):
        st = S[self.level] // 8
        groups = X[self.level] // 4
        slot = lax.shift_right_logical(iota((8, 128), 1), 3)
        ahead = 15 if self.level == 0 else 7

        def pack(f, c):
            for g in range(groups):
                up = down = None
                for k in range(4 * st):
                    v = self.field[f, 4 * g + k // st, pl.ds(8 * (k % st), 8), pl.ds(0, 128)]
                    v = pltpu.roll(v, 8 * k, 1) if k else v
                    up = v if up is None else jnp.where(slot == (k + ahead) % 16, v, up)
                    down = v if down is None else jnp.where(slot == k, v, down)
                self.send_up[f, g] = up
                self.send_down[f, g] = down
            return c

        lax.fori_loop(0, self.field.shape[0], pack, 0)
        for c in self.depth_copies():
            c.start()

    def depth_wait(self):
        for c in self.depth_copies():
            c.wait_recv()
        for c in self.depth_copies():
            c.wait_send()
        st = S[self.level] // 8
        groups = X[self.level] // 4
        lane = iota((8, 128), 1)
        even = lax.shift_right_logical(lane, 3) & 1 == 0
        fine = self.level == 0
        at = 0 if fine else self.lanes

        def unpack(f, c):
            for g in range(groups):
                below, above = self.got_up[f, g], self.got_down[f, g]
                merged = (jnp.where(even, above, below), jnp.where(even, below, above))
                for k in range(4 * st):
                    rows = pl.ds(8 * (k % st), 8)
                    x = 4 * g + k // st
                    both = pltpu.roll(merged[k % 2], (at - 8 * k) % 128, 1)
                    if fine:
                        self.field[f, x, rows, pl.ds(128, 128)] = both
                    else:
                        own = self.field[f, x, rows, pl.ds(0, 128)]
                        self.field[f, x, rows, pl.ds(0, 128)] = jnp.where(lane < 64, own, both)
            return c

        lax.fori_loop(0, self.field.shape[0], unpack, 0)


class Gather:
    def __init__(self, by_x, by_xy, plane, below, above, sems, relay=False):
        self.by_x, self.by_xy, self.plane, self.below, self.above = by_x, by_xy, plane, below, above
        self.ssem, self.rsem = sems
        self.relay = relay

    def ring(self, axis, src, dst, base, far=True):
        out = []
        me = lax.axis_index(axis)
        for i, m in enumerate((4, 3, 5, 2, 6, 1, 7) if far else (2, 6, 1, 7)):
            out.append(pltpu.make_async_remote_copy(
                src_ref=src, dst_ref=dst.at[me], send_sem=self.ssem.at[base + i], recv_sem=self.rsem.at[base + i],
                device_id={axis: lax.rem(me + m, SHARDS)}, device_id_type=MESH))
        return out

    def x_copies(self):
        return self.ring("gx", self.by_x.at[lax.axis_index("gx")], self.by_x, 0)

    def y_copies(self, far=True):
        return self.ring("gy", self.by_xy.at[lax.axis_index("gy")], self.by_xy, 7, far)

    def y_near(self):
        return self.y_copies(False)

    def y_far(self):
        out = []
        me = lax.axis_index("gy")
        for i, (whose, to) in enumerate(((6, 1), (6, 2), (2, 7))):
            block = self.by_xy.at[lax.rem(me + whose, SHARDS)]
            out.append(pltpu.make_async_remote_copy(
                src_ref=block, dst_ref=block, send_sem=self.ssem.at[11 + i], recv_sem=self.rsem.at[11 + i],
                device_id={"gy": lax.rem(me + to, SHARDS)}, device_id_type=MESH))
        return out

    def z_copies(self):
        return [
            pltpu.make_async_remote_copy(
                src_ref=self.plane, dst_ref=dst, send_sem=self.ssem.at[14 + i], recv_sem=self.rsem.at[14 + i],
                device_id=neighbour(gz=m), device_id_type=MESH)
            for i, (m, dst) in enumerate(((1, self.below), (-1, self.above)))]

    def wait(self, copies):
        for c in copies:
            c.wait_recv()
        for c in copies:
            c.wait_send()

    def x_start(self):
        for c in self.x_copies():
            c.start()

    def y_start(self):
        self.wait(self.x_copies())
        me = lax.axis_index("gy")
        for i in range(SHARDS):
            self.by_xy[me, i] = self.by_x[i]
        for c in self.y_near() if self.relay else self.y_copies():
            c.start()

    def y_more(self):
        self.wait(self.y_near())
        for c in self.y_far():
            c.start()

    def z_start(self):
        self.wait(self.y_far() if self.relay else self.y_copies())

        def put(i, c):
            gx, gy = i // SHARDS, i % SHARDS
            for f in range(self.plane.shape[0]):
                self.plane[f, gx, pl.ds(4 * gy, 4), :] = self.by_xy[gy, gx, f]
            return c

        lax.fori_loop(0, SHARDS * SHARDS, put, 0)
        for c in self.z_copies():
            c.start()

    def finish(self, outs):
        self.wait(self.z_copies())
        lane = iota((32, 128), 1)

        def put(gx, c):
            for f, out in enumerate(outs):
                own, low, high = self.plane[f, gx], self.below[f, gx], self.above[f, gx]
                for xx in range(4):
                    v = jnp.where(lane < 32, pltpu.roll(low, (-32 * xx) % 128, 1),
                                  jnp.where(lane < 64, pltpu.roll(own, (32 - 32 * xx) % 128, 1),
                                            pltpu.roll(high, (64 - 32 * xx) % 128, 1)))
                    out[HX[2] + 4 * gx + xx] = v
            return c

        lax.fori_loop(0, SHARDS, put, 0)


def kernel(keys, state, data, kappa, weight_x, weight_y, weight_z, out,
           f0, xd0, a0, n0, c1p, c1, r1, f1, xd1, a1, n1, c2, r2, f2, a2, n2, c3, r3, f3, a3, n3,
           res, t64, t256,
           p0a, p0b, p0c, p0d, pxa, pxb, pxc, pxd, pca, pcb, pcc, pcd, pra, prb, prc, prd, pya, pyb, pyc, pyd,
           gcx, gcxy, gcp, gcl, gch, grx, grxy, grp, grl, grh,
           ysent, ygot, csent, cgot, ssem, rsem):
    def sems(i):
        return ssem.at[i], rsem.at[i]

    bar = pltpu.get_barrier_semaphore()
    partners = [{"gx": m} for m in range(1, 8)] + [{"gy": m} for m in range(1, 8)] + [{"gz": 1}, {"gz": -1}]
    partners += [{"gx": a, "gy": b} for a in (1, -1) for b in (1, -1)]
    for p in partners:
        pl.semaphore_signal(bar, inc=1, device_id=neighbour(**p), device_id_type=MESH)

    for x in range(HX[2]):
        for at in (x, X[2] - 1 - x):
            f2[at] = jnp.zeros(f2.shape[1:], F32)
    for at in (0, X[3] - 1):
        f3[at] = jnp.zeros(f3.shape[1:], F32)

    for i, ref in enumerate((state, data, kappa, weight_x, weight_y, weight_z)):
        def load(x, c, i=i, ref=ref):
            f0[i, HX[0] + x, pl.ds(8, 16), pl.ds(0, 128)] = ref[x]
            return c
        lax.fori_loop(0, 16, load, 0)

    pl.semaphore_wait(bar, len(partners))

    halo0 = Halo(0, f0, 5, (p0a, p0b, p0c, p0d), sems(0), (ysent, ygot, csent, cgot))
    halox0 = Halo(0, xd0, 4, (pxa, pxb, pxc, pxd), sems(1))
    haloc1 = Halo(1, c1, 6, (pca, pcb, pcc, pcd), sems(2), (c1p,))
    halor1 = Halo(1, r1, 6, (pra, prb, prc, prd), sems(3))
    halox1 = Halo(1, xd1, 6, (pya, pyb, pyc, pyd), sems(4))
    gatherc = Gather(gcx, gcxy, gcp, gcl, gch, sems(5), True)
    gatherr = Gather(grx, grxy, grp, grl, grh, sems(6))

    halo0.plane_start()

    m01, m01_odd = halve(128, 128, 0, 128, 0), halve(128, 128, 0, 128, 0, True)
    both, odd = (0, 1), (1,)
    for i, (ref, xs, ys, m) in enumerate(((kappa, both, both, m01), (weight_x, odd, both, m01),
                                          (weight_y, both, odd, m01), (weight_z, both, both, m01_odd))):
        for cx in range(8):
            t64[pl.ds(8 * cx, 8), :] = pairs(ref, cx, 0, 8, xs, ys)
        t = dot(t64[...], m)
        for cx in range(8):
            c1[i, HX[1] + cx, pl.ds(8, 8), :] = t[8 * cx:8 * cx + 8]
            if i % 2:
                c1p[i // 2, HX[1] + cx, pl.ds(8, 8), :] = first[8 * cx:8 * cx + 8] + pltpu.roll(t, 64, 1)[8 * cx:8 * cx + 8]
        first = t
    gx = lax.axis_index("gx")
    for i, (xs, ys, flag) in enumerate(((both, both, False), (odd, both, False), (both, odd, False), (both, both, True))):
        t = jnp.zeros((4, 128), F32)
        for cx in range(4):
            t = t + dot(pairs(c1.at[i], 3 + cx, 8, 4, xs, ys), halve(128, 128, 0, 64, 32 * cx, flag))
        gcx[gx, i] = t

    gatherc.x_start()
    fill_noise(0, n0, keys)
    halo0.plane_wait()
    halo0.depth_start()
    gatherc.y_start()
    haloc1.plane_start()
    fill_noise(1, n1, keys)
    halo0.depth_wait()

    x0, b0 = f0.at[0], f0.at[1]
    derive(0, f0.at[2], f0.at[3], f0.at[4], f0.at[5], a0, n0, b0)
    sweeps(0, x0, b0, a0, n0, 0, 4)
    gatherc.y_more()
    residual_own(x0, b0, a0, res)
    for cx in range(8):
        t64[pl.ds(8 * cx, 8), :] = pairs(res, cx, 0, 8)
    t = dot(t64[...], m01)
    for cx in range(8):
        r1[0, HX[1] + cx, pl.ds(8, 8), :] = t[8 * cx:8 * cx + 8]
    halor1.plane_start()

    def keep0(x, c):
        xd0[0, x, pl.ds(8, 16), pl.ds(0, 128)] = x0[x, pl.ds(8, 16), pl.ds(0, 128)]
        return c
    lax.fori_loop(HX[0], HX[0] + 16, keep0, 0)
    haloc1.plane_wait()
    haloc1.depth_start()
    halor1.plane_wait()
    halor1.depth_start()
    halox0.plane_start()
    gatherc.z_start()
    haloc1.depth_wait()
    derive(1, c1.at[0], c1.at[1], c1.at[2], c1.at[3], a1, n1)
    halor1.depth_wait()

    b1 = r1.at[0]
    scale_rhs(1, b1, a1)
    sweeps(1, f1, b1, a1, n1, 0, 4, True)
    residual(1, f1, b1, a1, res, 8, 16)
    t = jnp.zeros((4, 128), F32)
    for cx in range(4):
        t = t + dot(pairs(res, cx, 0, 4), halve(128, 128, 0, 64, 32 * cx))
    grx[gx, 0] = t
    gatherr.x_start()

    def keep1(x, c):
        xd1[0, x, pl.ds(8, 8), :] = f1[x, pl.ds(8, 8), :]
        return c
    lax.fori_loop(HX[1], HX[1] + 8, keep1, 0)
    halox1.plane_start()
    halox0.plane_wait()
    halox0.depth_start()
    fill_noise(2, n2, keys)
    fill_noise(3, n3, keys)
    gatherr.y_start()
    gatherc.finish([c2.at[i] for i in range(4)])
    derive(2, c2.at[0], c2.at[1], c2.at[2], c2.at[3], a2, n2)
    halox1.plane_wait()
    halox1.depth_start()
    gatherr.z_start()
    m23, m23_odd = halve(128, 128, 0, 96, 0), halve(128, 128, 0, 96, 0, True)
    for i, (xs, ys, m) in enumerate(((both, both, m23), (odd, both, m23), (both, odd, m23), (both, both, m23_odd))):
        for cx in range(16):
            t256[pl.ds(16 * cx, 16), :] = pairs(c2.at[i], 2 + cx, 0, 16, xs, ys)
        t = dot(t256[...], m)
        for cx in range(16):
            c3[i, HX[3] + cx] = t[16 * cx:16 * cx + 16]
    derive(3, c3.at[0], c3.at[1], c3.at[2], c3.at[3], a3, n3)
    halox0.depth_wait()
    halox1.depth_wait()
    gatherr.finish([r2])

    scale_rhs(2, r2, a2)
    sweeps(2, f2, r2, a2, n2, 0, 0, True)
    residual(2, f2, r2, a2, res, 0, 32)
    for cx in range(16):
        t256[pl.ds(16 * cx, 16), :] = pairs(res, cx, 0, 16)
    t = dot(t256[...], m23)
    for cx in range(16):
        r3[HX[3] + cx] = t[16 * cx:16 * cx + 16]
    scale_rhs(3, r3, a3)
    sweeps(3, f3, r3, a3, n3, 0, 0, True)
    sweeps(3, f3, r3, a3, n3, 1, 0)
    for cx in range(16):
        t256[pl.ds(16 * cx, 16), :] = f3[HX[3] + cx]
    i3, i2 = iota((128, 128), 0), iota((128, 128), 1)
    t = dot(t256[...], ((lax.shift_right_logical(i2, 1) == i3) & (i2 < 96)).astype(F32))
    for cx in range(16):
        for dx in both:
            for dy in both:
                rows = pl.ds(dy, 16, stride=2)
                x = HX[2] + 2 * cx + dx
                f2[x, rows, :] = f2[x, rows, :] + t[16 * cx:16 * cx + 16]
    sweeps(2, f2, r2, a2, n2, 1, 0)

    gy = lax.axis_index("gy")
    z1 = relative_z(1, (128, 128))
    m21 = ((i3 == lax.shift_right_arithmetic(z1, 1) + 32) & (z1 >= -6) & (z1 < 70)).astype(F32)
    for j in range(10):
        v = f2[HX[2] + 4 * gx + (j - 3)]
        t256[pl.ds(16 * j, 16), :] = pltpu.roll(v, lax.rem(36 - 4 * gy, 32), 0)[:16]
    t = dot(t256[...], m21)
    for j in range(10):
        for dx in both:
            for dy in both:
                rows = pl.ds(dy, 12, stride=2)
                x = 2 * j + dx
                xd1[0, x, rows, :] = xd1[0, x, rows, :] + t[16 * j:16 * j + 12]
    sweeps(1, xd1.at[0], b1, a1, n1, 1, 5)

    z0 = relative_z(0, (128, 256))
    hit = iota((128, 256), 0) == (lax.shift_right_arithmetic(z0, 1) & 127)
    m10 = (hit & (z0 >= -4) & (z0 < 132)).astype(F32)
    for j in range(12):
        t256[pl.ds(16 * j, 16), :] = xd1[0, 4 + j, pl.ds(4, 16), :]
    t = dot(t256[pl.ds(0, 192), :], m10)
    for j in range(12):
        for dy in both:
            rows = pl.ds(dy, 16, stride=2)
            res[j, rows, :] = t[16 * j:16 * j + 16, :128]
            res[16 + j, rows, :] = t[16 * j:16 * j + 16, 128:]

    def add(j, c):
        for dx in both:
            x = 2 + 2 * j + dx
            xd0[0, x, :, pl.ds(0, 128)] = xd0[0, x, :, pl.ds(0, 128)] + res[j]
            xd0[0, x, :, pl.ds(128, 128)] = xd0[0, x, :, pl.ds(128, 128)] + res[16 + j]
        return c
    lax.fori_loop(0, 12, add, 0)
    sweeps(0, xd0.at[0], b0, a0, n0, 1, 3, halves=3)
    last_half(xd0.at[0], b0, a0, n0, 3, out)


def level_scratch(level, fields):
    shape = (X[level], S[level], W[level])
    return [pltpu.VMEM((n,) + shape if n else shape, F32) for n in fields]


def packs(level, n):
    return [pltpu.VMEM((n, X[level] // 4, 8, 128), F32)] * 4


def gathers(n):
    return [pltpu.VMEM((8, n, 4, 128), F32), pltpu.VMEM((8, 8, n, 4, 128), F32)] + [
        pltpu.VMEM((n, 8, 32, 128), F32)] * 3


def per_device(state, data_term, kappa, weight_x, weight_y, weight_z, noise_keys):
    scratch = (
        level_scratch(0, (6, 1, 8, 4)) + level_scratch(1, (2, 4, 1, 0, 1, 8, 4))
        + level_scratch(2, (4, 0, 0, 8, 4)) + level_scratch(3, (4, 0, 0, 8, 4))
        + [pltpu.VMEM((32, 32, 128), F32), pltpu.VMEM((64, 128), F32), pltpu.VMEM((256, 128), F32)]
        + packs(0, 6) + packs(0, 1) + packs(1, 4) + packs(1, 1) + packs(1, 1)
        + gathers(4) + gathers(1)
        + [pltpu.VMEM((2, 16, 32, 128), F32)] * 2 + [pltpu.VMEM((4, 64, 128), F32)] * 2
        + [pltpu.SemaphoreType.DMA((7, 16)), pltpu.SemaphoreType.DMA((7, 16))])
    return pl.pallas_call(
        kernel,
        out_shape=jax.ShapeDtypeStruct(state.shape, F32),
        in_specs=[pl.BlockSpec(memory_space=pltpu.SMEM)] + [pl.BlockSpec(memory_space=pltpu.VMEM)] * 6,
        out_specs=pl.BlockSpec(memory_space=pltpu.VMEM),
        scratch_shapes=scratch,
        compiler_params=pltpu.CompilerParams(
            collective_id=0, has_side_effects=True, vmem_limit_bytes=56 * 2**20),
    )(noise_keys.transpose(1, 2, 0), state, data_term, kappa, weight_x, weight_y, weight_z)


def solution(mesh):
    spec = P(*AXES)
    return jax.shard_map(
        per_device, mesh=mesh, in_specs=(spec,) * 6 + (P(),), out_specs=spec, check_vma=False)
```

```python
import functools
import math

import jax
import jax.numpy as jnp
from jax import lax
from jax.experimental import pallas as pl
from jax.experimental.pallas import tpu as pltpu
from jax.sharding import PartitionSpec as P

AXES = ("gx", "gy", "gz")
MESH = pl.DeviceIdType.MESH
F32 = jnp.float32
SHARDS = 8
GRID = ((128, 128, 1024), (64, 64, 512), (32, 32, 256), (16, 16, 128))
X = (28, 20, 40, 18)
S = (32, 24, 32, 16)
W = (256, 128, 128, 128)
HX = (6, 6, 4, 1)
HY = (8, 8, 0, 0)


def neighbour(**moves):
    return {a: lax.rem(lax.axis_index(a) + (m + SHARDS), SHARDS) for a, m in moves.items() if m}


def dot(a, b):
    return jnp.dot(a, b, precision=lax.Precision.HIGHEST, preferred_element_type=F32)


def iota(shape, dim):
    return lax.broadcasted_iota(jnp.int32, shape, dim)


def mixing(h):
    h = h ^ lax.shift_right_logical(h, jnp.int32(16))
    h = h * jnp.int32(-2048144789)
    h = h ^ lax.shift_right_logical(h, jnp.int32(13))
    h = h * jnp.int32(-1028477387)
    h = h ^ lax.shift_right_logical(h, jnp.int32(16))
    return h


def gaussian_like(index, key):
    first = mixing(index * jnp.int32(-1640531535) ^ key)
    second = mixing(first ^ jnp.int32(1759714724))
    steps = lax.shift_right_logical(first, jnp.int32(8)) + lax.shift_right_logical(second, jnp.int32(8))
    return steps.astype(F32) * (math.sqrt(6.0) / 16777216.0) - math.sqrt(6.0)


def relative_z(level, shape):
    lane = iota(shape, len(shape) - 1)
    if level == 0:
        return jnp.where(lane < 192, lane, lane - 256)
    if level == 1:
        return jnp.where(lane < 96, lane, lane - 128)
    return lane - (32 if level == 2 else 16)


def x_global(level, x):
    n = GRID[level][0]
    start = lax.axis_index("gx") * (n // SHARDS) if level < 2 else 0
    return (start + x - HX[level] + n) & (n - 1)


def yz_global(level):
    shape = (S[level], W[level])
    ny, nz = GRID[level][1:]
    start = lax.axis_index("gy") * (ny // SHARDS) if level < 2 else 0
    y = (iota(shape, 0) + (start - HY[level] + ny)) & (ny - 1)
    z = (relative_z(level, shape) + (lax.axis_index("gz") * (nz // SHARDS) + nz)) & (nz - 1)
    return y, z


def blocks(lo, count, size, body):
    def step(i, c):
        for ref, at, value in body(lo + i * size):
            ref[at] = value
        return c

    assert count % size == 0
    lax.fori_loop(0, count // size, step, 0)


def every(level):
    return ((2, 24, 4), (1, 18, 3), (4, 32, 4), (1, 16, 8))[level]


def span(level, depth):
    if level >= 2:
        return HX[level], GRID[level][0], 16
    own = GRID[level][0] // SHARDS
    lo, count = HX[level] - depth, own + 2 * depth
    if level == 0:
        return (lo, 24, 8) if depth >= 3 else (lo, 20, 10)
    return lo, count, count


def fill_noise(level, out, keys):
    nx, ny, nz = GRID[level]
    y, z = yz_global(level)
    plane = y * nz + z
    lo, count, _ = every(level)

    def row(x):
        index = plane + x_global(level, x) * (ny * nz)
        return [(out, (i, x), gaussian_like(index, keys[i // 2, i % 2, level])) for i in range(4)]

    blocks(lo, count, 1, row)


def derive(level, kap, wx, wy, wz, a, noise, rhs=None):
    nx, ny, nz = GRID[level]
    y, z = yz_global(level)
    y_first, y_last, z_first, z_last = y == 0, y == ny - 1, z == 0, z == nz - 1
    lo, count, size = every(level)

    def row(x0):
        stores = []
        for x in [x0 + i for i in range(size)]:
            xg = x_global(level, x)
            up, vp, sp = wx[x], wy[x], wz[x]
            um = jnp.where(xg == 0, 0.0, wx[x - 1])
            vm = jnp.where(y_first, 0.0, pltpu.roll(vp, 1, 0))
            sm = jnp.where(z_first, 0.0, pltpu.roll(sp, 1, 1))
            diag = kap[x] + up + um + vp + vm + sp + sm
            if level in (1, 3):
                diag = jnp.where(diag > 0.0, diag, 1.0)
            inv = 1.0 / diag
            root = lax.rsqrt(diag)
            values = (jnp.where(xg == nx - 1, 0.0, up) * inv, um * inv, jnp.where(y_last, 0.0, vp) * inv, vm * inv,
                      jnp.where(z_last, 0.0, sp) * inv, sm * inv, diag, inv)
            stores += [(a, (i, x), v) for i, v in enumerate(values)]
            stores += [(noise, (i, x), noise[i, x] * root) for i in range(4)]
            if rhs is not None:
                stores.append((rhs, x, rhs[x] * inv))
        return stores

    blocks(lo, count, size, row)


def scale_rhs(level, rhs, a):
    lo, count, size = every(level)
    blocks(lo, count, size, lambda x0: [(rhs, x0 + i, rhs[x0 + i] * a[7, x0 + i]) for i in range(size)])


def around(level, f, a, x0, size):
    s, w = S[level], W[level]
    v = [f[x0 + i] for i in range(-1, size + 1)]
    out = []
    for i in range(size):
        x, own = x0 + i, v[i + 1]
        t = a[0, x] * v[i + 2] + a[1, x] * v[i]
        u = a[2, x] * pltpu.roll(own, s - 1, 0) + a[3, x] * pltpu.roll(own, 1, 0)
        t = (t + u) + (a[4, x] * pltpu.roll(own, w - 1, 1) + a[5, x] * pltpu.roll(own, 1, 1))
        out.append((x, own, t))
    return out


def around_own(f, a, x0, size):
    rows, lanes, lane = pl.ds(8, 16), pl.ds(0, 128), iota((16, 128), 1)
    v = [f[x0 + i, rows, lanes] for i in range(-1, size + 1)]
    out = []
    for i in range(size):
        x, own = x0 + i, v[i + 1]
        side = f[x, rows, pl.ds(128, 128)]
        t = a[0, x, rows, lanes] * v[i + 2] + a[1, x, rows, lanes] * v[i]
        u = a[2, x, rows, lanes] * f[x, pl.ds(9, 16), lanes] + a[3, x, rows, lanes] * f[x, pl.ds(7, 16), lanes]
        after = jnp.where(lane == 127, pltpu.roll(side, 127, 1), pltpu.roll(own, 127, 1))
        before = jnp.where(lane == 0, pltpu.roll(side, 1, 1), pltpu.roll(own, 1, 1))
        out.append((x, own, (t + u) + (a[4, x, rows, lanes] * after + a[5, x, rows, lanes] * before)))
    return out


def last_half(f, rhs, a, noise, sweep, out):
    rows, lanes = pl.ds(8, 16), pl.ds(0, 128)

    def block(x0):
        masks = colored(0, x0, 1, (16, 128))
        return [(out, x - HX[0], jnp.where(masks[i % 2], rhs[x, rows, lanes] + t + noise[sweep, x, rows, lanes], own))
                for i, (x, own, t) in enumerate(around_own(f, a, x0, 8))]

    blocks(HX[0], 16, 8, block)


def residual_own(f, rhs, a, out):
    rows, lanes = pl.ds(8, 16), pl.ds(0, 128)

    def block(x0):
        return [(out, (x - HX[0], pl.ds(0, 16), slice(None)), a[6, x, rows, lanes] * (rhs[x, rows, lanes] + t - v))
                for x, v, t in around_own(f, a, x0, 8)]

    blocks(HX[0], 16, 8, block)


def colored(level, x0, color, shape=None):
    shape = shape or (S[level], W[level])
    odd = (iota(shape, 0) + iota(shape, 1) + (x0 + (HX[level] + HY[level]))) & 1
    return odd == color, odd != color


def half_sweep(level, f, rhs, a, noise, sweep, color, depth):
    lo, count, size = span(level, depth)

    def rows(x0):
        masks = colored(level, x0, color)
        return [(f, x, jnp.where(masks[i % 2], rhs[x] + t + noise[sweep, x], own))
                for i, (x, own, t) in enumerate(around(level, f, a, x0, size))]

    blocks(lo, count, size, rows)


def first_half(level, f, rhs, noise, sweep, depth):
    lo, count, size = span(level, depth)

    def rows(x0):
        masks = colored(level, x0, 0)
        return [(f, x0 + i, jnp.where(masks[i % 2], rhs[x0 + i] + noise[sweep, x0 + i], 0.0)) for i in range(size)]

    blocks(lo, count, size, rows)


def sweeps(level, f, rhs, a, noise, leg, depth, from_zero=False, halves=4):
    for i in range(halves):
        if from_zero and i == 0:
            first_half(level, f, rhs, noise, 0, depth)
        else:
            half_sweep(level, f, rhs, a, noise, 2 * leg + i // 2, i % 2, depth - i)


def residual(level, f, rhs, a, out, y0, y1):
    lo, count, size = span(level, 0)
    size = min(size, 8)

    def rows(x0):
        return [(out, (x - lo, pl.ds(0, y1 - y0), slice(None)), (a[6, x] * (rhs[x] + t - v))[y0:y1, 0:128])
                for x, v, t in around(level, f, a, x0, size)]

    blocks(lo, count, size, rows)


def pairs(ref, cx, y0, n, xs=(0, 1), ys=(0, 1)):
    total = None
    for dx in xs:
        for dy in ys:
            v = ref[2 * cx + dx, pl.ds(y0 + dy, n, stride=2), :]
            total = v if total is None else total + v
    return total


def halve(rows, cols, start_r, limit, start_c, odd=False):
    r, c = iota((rows, cols), 0) - start_r, iota((rows, cols), 1) - start_c
    hit = (lax.shift_right_arithmetic(r, 1) == c) & (r >= 0) & (r < limit)
    if odd:
        hit = hit & (r & 1 == 1)
    return hit.astype(F32)


class Halo:
    def __init__(self, level, field, depth, packs, sems, tight=None):
        self.level, self.field, self.depth = level, field, depth
        self.send_up, self.send_down, self.got_up, self.got_down = packs
        self.ssem, self.rsem = sems
        self.tight = tight
        self.n = GRID[level][0] // SHARDS
        self.lanes = GRID[level][2] // SHARDS

    def plane_copies(self):
        n, d, hx, hy = self.n, self.depth, HX[self.level], HY[self.level]
        out = []
        moves = [(1, 0), (-1, 0), (0, 1), (0, -1), (1, 1), (1, -1), (-1, 1), (-1, -1)]
        for i, (mx, my) in enumerate(moves):
            sx, dx, lx = {0: (hx, hx, n), 1: (hx + n - d, hx - d, d), -1: (hx, hx + n, d)}[mx]
            sy, dy, ly = {0: (hy, hy, n), 1: (hy + n - 8, hy - 8, 8), -1: (hy, hy + n, 8)}[my]
            src = self.field.at[:, pl.ds(sx, lx), pl.ds(sy, ly), pl.ds(0, 128)]
            dst = self.field.at[:, pl.ds(dx, lx), pl.ds(dy, ly), pl.ds(0, 128)]
            if self.level == 1 and self.tight:
                src = self.tight[0].at[:, pl.ds(sx, lx), pl.ds(sy, ly), :]
                dst = self.tight[0].at[:, pl.ds(dx, lx), pl.ds(dy, ly), :]
            elif self.tight and my:
                sent, got, j = self.tight[:2] + (i - 2,) if i < 4 else self.tight[2:] + (i - 4,)
                src, dst = sent.at[j], got.at[j]
            out.append(pltpu.make_async_remote_copy(
                src_ref=src, dst_ref=dst,
                send_sem=self.ssem.at[i], recv_sem=self.rsem.at[i],
                device_id=neighbour(gx=mx, gy=my), device_id_type=MESH))
        return out

    def depth_copies(self):
        out = []
        for i, (mz, src, dst) in enumerate(((1, self.send_up, self.got_up), (-1, self.send_down, self.got_down))):
            out.append(pltpu.make_async_remote_copy(
                src_ref=src, dst_ref=dst, send_sem=self.ssem.at[8 + i], recv_sem=self.rsem.at[8 + i],
                device_id=neighbour(gz=mz), device_id_type=MESH))
        return out

    def plane_start(self):
        copies = self.plane_copies()
        if self.tight and self.level == 0:
            for c in copies[:2]:
                c.start()
            self.stage(True)
            for c in copies[2:]:
                c.start()
        else:
            for c in copies:
                c.start()

    def stage(self, out):
        sent_y, got_y, sent_xy, got_xy = self.tight
        fields, hx = self.field.shape[0], HX[0]

        def face(x, c):
            for j in range(2):
                for f in range(fields):
                    rows = pl.ds(5 * f, 5)
                    if out:
                        sent_y[j, x, rows, :] = self.field[f, hx + x, pl.ds(8 if j else 19, 5), pl.ds(0, 128)]
                    else:
                        self.field[f, hx + x, pl.ds(24 if j else 3, 5), pl.ds(0, 128)] = got_y[j, x, rows, :]
            return c

        def corner(j):
            at = 0
            for i in range(4):
                n = 4 - i
                xs, xd = (6 + i, 22 + i) if j >= 2 else (21 - i, 5 - i)
                ys, yd = (8, 24) if j % 2 else (24 - n, 8 - n)
                for f in range(fields):
                    rows = pl.ds(at, n)
                    if out:
                        sent_xy[j, rows, :] = self.field[f, xs, pl.ds(ys, n), pl.ds(0, 128)]
                    else:
                        self.field[f, xd, pl.ds(yd, n), pl.ds(0, 128)] = got_xy[j, rows, :]
                    at += n

        lax.fori_loop(0, 16, face, 0)
        for j in range(4):
            corner(j)

    def plane_wait(self):
        for c in self.plane_copies():
            c.wait_recv()
        for c in self.plane_copies():
            c.wait_send()
        if self.tight and self.level == 0:
            self.stage(False)
        elif self.tight:
            self.split()

    def split(self):
        both = self.tight[0]

        def rows(x0):
            return [(self.field, (2 * i + j, x), pltpu.roll(both[i, x], 64, 1) if j else both[i, x])
                    for x in (x0, x0 + 1) for i in range(2) for j in range(2)]

        blocks(0, X[1], 2, rows)

    def depth_start(self):
        st = S[self.level] // 8
        groups = X[self.level] // 4
        slot = lax.shift_right_logical(iota((8, 128), 1), 3)
        ahead = 15 if self.level == 0 else 7

        def pack(f, c):
            for g in range(groups):
                up = down = None
                for k in range(4 * st):
                    v = self.field[f, 4 * g + k // st, pl.ds(8 * (k % st), 8), pl.ds(0, 128)]
                    v = pltpu.roll(v, 8 * k, 1) if k else v
                    up = v if up is None else jnp.where(slot == (k + ahead) % 16, v, up)
                    down = v if down is None else jnp.where(slot == k, v, down)
                self.send_up[f, g] = up
                self.send_down[f, g] = down
            return c

        lax.fori_loop(0, self.field.shape[0], pack, 0)
        for c in self.depth_copies():
            c.start()

    def depth_wait(self):
        for c in self.depth_copies():
            c.wait_recv()
        for c in self.depth_copies():
            c.wait_send()
        st = S[self.level] // 8
        groups = X[self.level] // 4
        lane = iota((8, 128), 1)
        even = lax.shift_right_logical(lane, 3) & 1 == 0
        fine = self.level == 0
        at = 0 if fine else self.lanes

        def unpack(f, c):
            for g in range(groups):
                below, above = self.got_up[f, g], self.got_down[f, g]
                merged = (jnp.where(even, above, below), jnp.where(even, below, above))
                for k in range(4 * st):
                    rows = pl.ds(8 * (k % st), 8)
                    x = 4 * g + k // st
                    both = pltpu.roll(merged[k % 2], (at - 8 * k) % 128, 1)
                    if fine:
                        self.field[f, x, rows, pl.ds(128, 128)] = both
                    else:
                        own = self.field[f, x, rows, pl.ds(0, 128)]
                        self.field[f, x, rows, pl.ds(0, 128)] = jnp.where(lane < 64, own, both)
            return c

        lax.fori_loop(0, self.field.shape[0], unpack, 0)


class Gather:
    def __init__(self, by_x, by_xy, plane, below, above, sems, relay=False):
        self.by_x, self.by_xy, self.plane, self.below, self.above = by_x, by_xy, plane, below, above
        self.ssem, self.rsem = sems
        self.relay = relay

    def ring(self, axis, src, dst, base, far=True):
        out = []
        me = lax.axis_index(axis)
        for i, m in enumerate((4, 3, 5, 2, 6, 1, 7) if far else (2, 6, 1, 7)):
            out.append(pltpu.make_async_remote_copy(
                src_ref=src, dst_ref=dst.at[me], send_sem=self.ssem.at[base + i], recv_sem=self.rsem.at[base + i],
                device_id={axis: lax.rem(me + m, SHARDS)}, device_id_type=MESH))
        return out

    def x_copies(self):
        return self.ring("gx", self.by_x.at[lax.axis_index("gx")], self.by_x, 0)

    def y_copies(self, far=True):
        return self.ring("gy", self.by_xy.at[lax.axis_index("gy")], self.by_xy, 7, far)

    def y_near(self):
        return self.y_copies(False)

    def y_far(self):
        out = []
        me = lax.axis_index("gy")
        for i, (whose, to) in enumerate(((6, 1), (6, 2), (2, 7))):
            block = self.by_xy.at[lax.rem(me + whose, SHARDS)]
            out.append(pltpu.make_async_remote_copy(
                src_ref=block, dst_ref=block, send_sem=self.ssem.at[11 + i], recv_sem=self.rsem.at[11 + i],
                device_id={"gy": lax.rem(me + to, SHARDS)}, device_id_type=MESH))
        return out

    def z_copies(self):
        return [
            pltpu.make_async_remote_copy(
                src_ref=self.plane, dst_ref=dst, send_sem=self.ssem.at[14 + i], recv_sem=self.rsem.at[14 + i],
                device_id=neighbour(gz=m), device_id_type=MESH)
            for i, (m, dst) in enumerate(((1, self.below), (-1, self.above)))]

    def wait(self, copies):
        for c in copies:
            c.wait_recv()
        for c in copies:
            c.wait_send()

    def x_start(self):
        for c in self.x_copies():
            c.start()

    def y_start(self):
        self.wait(self.x_copies())
        me = lax.axis_index("gy")
        for i in range(SHARDS):
            self.by_xy[me, i] = self.by_x[i]
        for c in self.y_near() if self.relay else self.y_copies():
            c.start()

    def y_more(self):
        self.wait(self.y_near())
        for c in self.y_far():
            c.start()

    def z_start(self):
        self.wait(self.y_far() if self.relay else self.y_copies())

        def put(i, c):
            gx, gy = i // SHARDS, i % SHARDS
            for f in range(self.plane.shape[0]):
                self.plane[f, gx, pl.ds(4 * gy, 4), :] = self.by_xy[gy, gx, f]
            return c

        lax.fori_loop(0, SHARDS * SHARDS, put, 0)
        for c in self.z_copies():
            c.start()

    def finish(self, outs):
        self.wait(self.z_copies())
        lane = iota((32, 128), 1)

        def put(gx, c):
            for f, out in enumerate(outs):
                own, low, high = self.plane[f, gx], self.below[f, gx], self.above[f, gx]
                for xx in range(4):
                    v = jnp.where(lane < 32, pltpu.roll(low, (-32 * xx) % 128, 1),
                                  jnp.where(lane < 64, pltpu.roll(own, (32 - 32 * xx) % 128, 1),
                                            pltpu.roll(high, (64 - 32 * xx) % 128, 1)))
                    out[HX[2] + 4 * gx + xx] = v
            return c

        lax.fori_loop(0, SHARDS, put, 0)


def kernel(keys, state, data, kappa, weight_x, weight_y, weight_z, out,
           f0, xd0, a0, n0, c1p, c1, r1, f1, xd1, a1, n1, c2, r2, f2, a2, n2, c3, r3, f3, a3, n3,
           res, t64, t256,
           p0a, p0b, p0c, p0d, pxa, pxb, pxc, pxd, pca, pcb, pcc, pcd, pra, prb, prc, prd, pya, pyb, pyc, pyd,
           gcx, gcxy, gcp, gcl, gch, grx, grxy, grp, grl, grh,
           ysent, ygot, csent, cgot, ssem, rsem):
    def sems(i):
        return ssem.at[i], rsem.at[i]

    bar = pltpu.get_barrier_semaphore()
    partners = [{"gx": m} for m in range(1, 8)] + [{"gy": m} for m in range(1, 8)] + [{"gz": 1}, {"gz": -1}]
    partners += [{"gx": a, "gy": b} for a in (1, -1) for b in (1, -1)]
    for p in partners:
        pl.semaphore_signal(bar, inc=1, device_id=neighbour(**p), device_id_type=MESH)

    for x in range(HX[2]):
        for at in (x, X[2] - 1 - x):
            f2[at] = jnp.zeros(f2.shape[1:], F32)
    for at in (0, X[3] - 1):
        f3[at] = jnp.zeros(f3.shape[1:], F32)

    for i, ref in enumerate((state, data, kappa, weight_x, weight_y, weight_z)):
        def load(x, c, i=i, ref=ref):
            f0[i, HX[0] + x, pl.ds(8, 16), pl.ds(0, 128)] = ref[x]
            return c
        lax.fori_loop(0, 16, load, 0)

    pl.semaphore_wait(bar, len(partners))

    halo0 = Halo(0, f0, 5, (p0a, p0b, p0c, p0d), sems(0), (ysent, ygot, csent, cgot))
    halox0 = Halo(0, xd0, 4, (pxa, pxb, pxc, pxd), sems(1))
    haloc1 = Halo(1, c1, 6, (pca, pcb, pcc, pcd), sems(2), (c1p,))
    halor1 = Halo(1, r1, 6, (pra, prb, prc, prd), sems(3))
    halox1 = Halo(1, xd1, 6, (pya, pyb, pyc, pyd), sems(4))
    gatherc = Gather(gcx, gcxy, gcp, gcl, gch, sems(5), True)
    gatherr = Gather(grx, grxy, grp, grl, grh, sems(6))

    halo0.plane_start()

    m01, m01_odd = halve(128, 128, 0, 128, 0), halve(128, 128, 0, 128, 0, True)
    both, odd = (0, 1), (1,)
    for i, (ref, xs, ys, m) in enumerate(((kappa, both, both, m01), (weight_x, odd, both, m01),
                                          (weight_y, both, odd, m01), (weight_z, both, both, m01_odd))):
        for cx in range(8):
            t64[pl.ds(8 * cx, 8), :] = pairs(ref, cx, 0, 8, xs, ys)
        t = dot(t64[...], m)
        for cx in range(8):
            c1[i, HX[1] + cx, pl.ds(8, 8), :] = t[8 * cx:8 * cx + 8]
            if i % 2:
                c1p[i // 2, HX[1] + cx, pl.ds(8, 8), :] = first[8 * cx:8 * cx + 8] + pltpu.roll(t, 64, 1)[8 * cx:8 * cx + 8]
        first = t
    gx = lax.axis_index("gx")
    for i, (xs, ys, flag) in enumerate(((both, both, False), (odd, both, False), (both, odd, False), (both, both, True))):
        t = jnp.zeros((4, 128), F32)
        for cx in range(4):
            t = t + dot(pairs(c1.at[i], 3 + cx, 8, 4, xs, ys), halve(128, 128, 0, 64, 32 * cx, flag))
        gcx[gx, i] = t

    gatherc.x_start()
    fill_noise(0, n0, keys)
    halo0.plane_wait()
    halo0.depth_start()
    gatherc.y_start()
    haloc1.plane_start()
    fill_noise(1, n1, keys)
    halo0.depth_wait()

    x0, b0 = f0.at[0], f0.at[1]
    derive(0, f0.at[2], f0.at[3], f0.at[4], f0.at[5], a0, n0, b0)
    sweeps(0, x0, b0, a0, n0, 0, 4)
    gatherc.y_more()
    residual_own(x0, b0, a0, res)
    for cx in range(8):
        t64[pl.ds(8 * cx, 8), :] = pairs(res, cx, 0, 8)
    t = dot(t64[...], m01)
    for cx in range(8):
        r1[0, HX[1] + cx, pl.ds(8, 8), :] = t[8 * cx:8 * cx + 8]
    halor1.plane_start()

    def keep0(x, c):
        xd0[0, x, pl.ds(8, 16), pl.ds(0, 128)] = x0[x, pl.ds(8, 16), pl.ds(0, 128)]
        return c
    lax.fori_loop(HX[0], HX[0] + 16, keep0, 0)
    haloc1.plane_wait()
    haloc1.depth_start()
    halor1.plane_wait()
    halor1.depth_start()
    halox0.plane_start()
    gatherc.z_start()
    haloc1.depth_wait()
    derive(1, c1.at[0], c1.at[1], c1.at[2], c1.at[3], a1, n1)
    halor1.depth_wait()

    b1 = r1.at[0]
    scale_rhs(1, b1, a1)
    sweeps(1, f1, b1, a1, n1, 0, 4, True)
    residual(1, f1, b1, a1, res, 8, 16)
    t = jnp.zeros((4, 128), F32)
    for cx in range(4):
        t = t + dot(pairs(res, cx, 0, 4), halve(128, 128, 0, 64, 32 * cx))
    grx[gx, 0] = t
    gatherr.x_start()

    def keep1(x, c):
        xd1[0, x, pl.ds(8, 8), :] = f1[x, pl.ds(8, 8), :]
        return c
    lax.fori_loop(HX[1], HX[1] + 8, keep1, 0)
    halox1.plane_start()
    halox0.plane_wait()
    halox0.depth_start()
    fill_noise(2, n2, keys)
    fill_noise(3, n3, keys)
    gatherr.y_start()
    gatherc.finish([c2.at[i] for i in range(4)])
    derive(2, c2.at[0], c2.at[1], c2.at[2], c2.at[3], a2, n2)
    halox1.plane_wait()
    halox1.depth_start()
    gatherr.z_start()
    m23, m23_odd = halve(128, 128, 0, 96, 0), halve(128, 128, 0, 96, 0, True)
    for i, (xs, ys, m) in enumerate(((both, both, m23), (odd, both, m23), (both, odd, m23), (both, both, m23_odd))):
        for cx in range(16):
            t256[pl.ds(16 * cx, 16), :] = pairs(c2.at[i], 2 + cx, 0, 16, xs, ys)
        t = dot(t256[...], m)
        for cx in range(16):
            c3[i, HX[3] + cx] = t[16 * cx:16 * cx + 16]
    derive(3, c3.at[0], c3.at[1], c3.at[2], c3.at[3], a3, n3)
    halox0.depth_wait()
    halox1.depth_wait()
    gatherr.finish([r2])

    scale_rhs(2, r2, a2)
    sweeps(2, f2, r2, a2, n2, 0, 0, True)
    residual(2, f2, r2, a2, res, 0, 32)
    for cx in range(16):
        t256[pl.ds(16 * cx, 16), :] = pairs(res, cx, 0, 16)
    t = dot(t256[...], m23)
    for cx in range(16):
        r3[HX[3] + cx] = t[16 * cx:16 * cx + 16]
    scale_rhs(3, r3, a3)
    sweeps(3, f3, r3, a3, n3, 0, 0, True)
    sweeps(3, f3, r3, a3, n3, 1, 0)
    for cx in range(16):
        t256[pl.ds(16 * cx, 16), :] = f3[HX[3] + cx]
    i3, i2 = iota((128, 128), 0), iota((128, 128), 1)
    t = dot(t256[...], ((lax.shift_right_logical(i2, 1) == i3) & (i2 < 96)).astype(F32))
    for cx in range(16):
        for dx in both:
            for dy in both:
                rows = pl.ds(dy, 16, stride=2)
                x = HX[2] + 2 * cx + dx
                f2[x, rows, :] = f2[x, rows, :] + t[16 * cx:16 * cx + 16]
    sweeps(2, f2, r2, a2, n2, 1, 0)

    gy = lax.axis_index("gy")
    z1 = relative_z(1, (128, 128))
    m21 = ((i3 == lax.shift_right_arithmetic(z1, 1) + 32) & (z1 >= -6) & (z1 < 70)).astype(F32)
    for j in range(10):
        v = f2[HX[2] + 4 * gx + (j - 3)]
        t256[pl.ds(16 * j, 16), :] = pltpu.roll(v, lax.rem(36 - 4 * gy, 32), 0)[:16]
    t = dot(t256[...], m21)
    for j in range(10):
        for dx in both:
            for dy in both:
                rows = pl.ds(dy, 12, stride=2)
                x = 2 * j + dx
                xd1[0, x, rows, :] = xd1[0, x, rows, :] + t[16 * j:16 * j + 12]
    sweeps(1, xd1.at[0], b1, a1, n1, 1, 5)

    z0 = relative_z(0, (128, 256))
    hit = iota((128, 256), 0) == (lax.shift_right_arithmetic(z0, 1) & 127)
    m10 = (hit & (z0 >= -4) & (z0 < 132)).astype(F32)
    for j in range(12):
        t256[pl.ds(16 * j, 16), :] = xd1[0, 4 + j, pl.ds(4, 16), :]
    t = dot(t256[pl.ds(0, 192), :], m10)
    for j in range(12):
        for dy in both:
            rows = pl.ds(dy, 16, stride=2)
            res[j, rows, :] = t[16 * j:16 * j + 16, :128]
            res[16 + j, rows, :] = t[16 * j:16 * j + 16, 128:]

    def add(j, c):
        for dx in both:
            x = 2 + 2 * j + dx
            xd0[0, x, :, pl.ds(0, 128)] = xd0[0, x, :, pl.ds(0, 128)] + res[j]
            xd0[0, x, :, pl.ds(128, 128)] = xd0[0, x, :, pl.ds(128, 128)] + res[16 + j]
        return c
    lax.fori_loop(0, 12, add, 0)
    sweeps(0, xd0.at[0], b0, a0, n0, 1, 3, halves=3)
    last_half(xd0.at[0], b0, a0, n0, 3, out)


def level_scratch(level, fields):
    shape = (X[level], S[level], W[level])
    return [pltpu.VMEM((n,) + shape if n else shape, F32) for n in fields]


def packs(level, n):
    return [pltpu.VMEM((n, X[level] // 4, 8, 128), F32)] * 4


def gathers(n):
    return [pltpu.VMEM((8, n, 4, 128), F32), pltpu.VMEM((8, 8, n, 4, 128), F32)] + [
        pltpu.VMEM((n, 8, 32, 128), F32)] * 3


def per_device(state, data_term, kappa, weight_x, weight_y, weight_z, noise_keys):
    scratch = (
        level_scratch(0, (6, 1, 8, 4)) + level_scratch(1, (2, 4, 1, 0, 1, 8, 4))
        + level_scratch(2, (4, 0, 0, 8, 4)) + level_scratch(3, (4, 0, 0, 8, 4))
        + [pltpu.VMEM((32, 32, 128), F32), pltpu.VMEM((64, 128), F32), pltpu.VMEM((256, 128), F32)]
        + packs(0, 6) + packs(0, 1) + packs(1, 4) + packs(1, 1) + packs(1, 1)
        + gathers(4) + gathers(1)
        + [pltpu.VMEM((2, 16, 32, 128), F32)] * 2 + [pltpu.VMEM((4, 64, 128), F32)] * 2
        + [pltpu.SemaphoreType.DMA((7, 16)), pltpu.SemaphoreType.DMA((7, 16))])
    return pl.pallas_call(
        kernel,
        out_shape=jax.ShapeDtypeStruct(state.shape, F32),
        in_specs=[pl.BlockSpec(memory_space=pltpu.SMEM)] + [pl.BlockSpec(memory_space=pltpu.VMEM)] * 6,
        out_specs=pl.BlockSpec(memory_space=pltpu.VMEM),
        scratch_shapes=scratch,
        compiler_params=pltpu.CompilerParams(
            collective_id=0, has_side_effects=True, vmem_limit_bytes=56 * 2**20),
    )(noise_keys.transpose(1, 2, 0), state, data_term, kappa, weight_x, weight_y, weight_z)


def solution(mesh):
    spec = P(*AXES)
    return jax.shard_map(
        per_device, mesh=mesh, in_specs=(spec,) * 6 + (P(),), out_specs=spec, check_vma=False)
```
